128 devices in a mesh: dp: 8 (over y, x_hi), ctx: 16 (over x_lo, z, core).
Axes of the slice: x: 4 (x_hi: 2, x_lo: 2; x = x_hi * 2 + x_lo), y: 4, z: 4, core: 2. Of those that a mesh axis runs over, the one named last changes fastest.
Arguments:
- teacher_query: bfloat16 [8, 2048, 2048], P('dp', 'ctx'), may hold values from -20 to 20
- teacher_key: bfloat16 [8, 2048, 2048], P('dp', 'ctx'), may hold values from -20 to 20
- student_hidden: bfloat16 [8, 2048, 1536], P('dp', 'ctx'), may hold values from -20 to 20
- weight_query: bfloat16 [1536, 768], replicated, may hold values from -0.15625 to 0.15625
- weight_key: bfloat16 [1536, 768], replicated, may hold values from -0.15625 to 0.15625
- doc_lengths: int32 [8, 8], P('dp'), may hold values from 1 to 256, as said below
Outputs:
- group_loss: float32 [8], P('dp')
- grad_hidden: bfloat16 [8, 2048, 1536], P('dp', 'ctx')
- grad_wq: float32 [1536, 768], P('ctx')
- grad_wk: float32 [1536, 768], P('ctx')
The draws below stay inside these ranges and needn't reach their ends.
Inputs may be any that keep to these rules, and one draw needn't show every extreme that they name: `doc_lengths`: each group's 8 lengths are positive and sum to 1984 (the positions after them are padding); the last document is the longest, exactly 256.
All inputs are finite; a program needn't handle non-finite values.
Results may differ from the reference program's by a relative error of at most 0.015.
The reference program's roundings to bfloat16 on the way (of `student_queries`, `student_keys` and `weights`) count: a program that leaves them out, or rounds other values in their place, can miss the bound.
Values may be sent and summed in bfloat16 or wider, within the bound.
A program may use at most 128 MiB of HBM per device.

```python
import math
import jax
import jax.numpy as jnp
from jax import lax

H = 16
TDH = 128
SDH = 48
DS = 1536
DOCS = 8
R = 128
GROUPS = 8
L = 2048
MOST = 256
TW = 2048
SW = 768


def drawn_rows(key, shape):
    return 0.5 * jnp.clip(jax.random.normal(key, shape, jnp.float32), -4.0, 4.0)


def draw_teacher_query(key, part):
    key = jax.random.fold_in(key, 5)
    return drawn_rows(key, (GROUPS, L, TW)).astype(jnp.bfloat16)


def draw_teacher_key(key, part):
    key = jax.random.fold_in(key, 7)
    return drawn_rows(key, (GROUPS, L, TW)).astype(jnp.bfloat16)


def draw_student_hidden(key, part):
    key = jax.random.fold_in(key, 9)
    return drawn_rows(key, (GROUPS, L, DS)).astype(jnp.bfloat16)


def draw_doc_lengths(key, part):
    key = jax.random.fold_in(key, 11)
    picks = jax.random.randint(key, (GROUPS, R // 2), 0, DOCS - 1).astype(jnp.int32)
    labels = jnp.arange(DOCS - 1, dtype=jnp.int32)
    counts = jnp.sum((picks[:, :, None] == labels[None, None, :]).astype(jnp.int32), axis=1).astype(jnp.int32)
    front = (MOST - counts).astype(jnp.int32)
    last = jnp.full((GROUPS, 1), MOST, jnp.int32)
    return jnp.concatenate([front, last], axis=1).astype(jnp.int32)


def scatter_about(own_key, extent, scale, limit, held_as=jnp.bfloat16):
    entries = jax.random.normal(own_key, extent, jnp.float32) * scale
    return jnp.minimum(jnp.maximum(entries, -limit), limit).astype(held_as)


def setup_inputs(seed: int = 0) -> dict:
    arg_keys = jax.random.split(jax.random.key(seed), 7)
    return {
        "teacher_query": draw_teacher_query(jax.random.fold_in(arg_keys[6], 71), 0),
        "teacher_key": draw_teacher_key(jax.random.fold_in(arg_keys[6], 71), 0),
        "student_hidden": draw_student_hidden(jax.random.fold_in(arg_keys[6], 71), 0),
        "weight_query": scatter_about(arg_keys[3], (DS, SW), DS ** -0.5, 0.15625),
        "weight_key": scatter_about(arg_keys[4], (DS, SW), DS ** -0.5, 0.15625),
        "doc_lengths": draw_doc_lengths(jax.random.fold_in(arg_keys[6], 71), 0),
    }


loss_scale = 1048576.0
negative_big = -1e+30

def document_ids(positions, bounds):
    return lax.optimization_barrier(jnp.sum((positions[:, None] >= bounds[None, :]).astype(jnp.int32), axis=1)).astype(jnp.int32)

def log_total(scores, allowed, row_valid):
    highest = lax.optimization_barrier(jnp.max(jnp.where(allowed, scores, negative_big), axis=1))
    summed = lax.optimization_barrier(jnp.sum(jnp.where(allowed, jnp.exp(scores - highest[:, None]), 0.0), axis=1))
    return jnp.where(row_valid, highest + jnp.log(jnp.where(row_valid, summed, 1.0)), 0.0)

def head_terms(teacher_head, student_head, allowed, row_valid, coefficient):
    teacher_scores = jnp.dot(teacher_head, teacher_head.T, preferred_element_type=jnp.float32) * (1.0 / math.sqrt(TDH))
    student_scores = jnp.dot(student_head, student_head.T, preferred_element_type=jnp.float32) * (1.0 / math.sqrt(SDH))
    teacher_total = log_total(teacher_scores, allowed, row_valid)
    student_total = log_total(student_scores, allowed, row_valid)
    teacher_prob = jnp.where(allowed, jnp.exp(teacher_scores - teacher_total[:, None]), 0.0)
    student_prob = jnp.where(allowed, jnp.exp(student_scores - student_total[:, None]), 0.0)
    teacher_back = jnp.where(allowed, jnp.exp(teacher_scores - teacher_total[None, :]), 0.0)
    student_back = jnp.where(allowed, jnp.exp(student_scores - student_total[None, :]), 0.0)
    weights = (coefficient * (student_prob - teacher_prob + (student_back - teacher_back))).astype(jnp.bfloat16)
    grad_head = jnp.dot(weights, student_head, preferred_element_type=jnp.float32) * (1.0 / math.sqrt(SDH))
    divergence = jnp.sum(jnp.where(allowed, teacher_prob * (teacher_scores - teacher_total[:, None] - (student_scores - student_total[:, None])), 0.0))
    return (grad_head, divergence)

def relation(teacher_rows, student_rows, allowed, row_valid, coefficient):
    teacher_heads = teacher_rows.reshape(L, H, TDH).transpose(1, 0, 2)
    student_heads = student_rows.reshape(L, H, SDH).transpose(1, 0, 2)

    def one_head(pair):
        return head_terms(pair[0], pair[1], allowed, row_valid, coefficient)
    grads, divergences = lax.map(one_head, (teacher_heads, student_heads))
    return (grads.transpose(1, 0, 2).reshape(L, H * SDH), jnp.sum(divergences))

def reference(teacher_query, teacher_key, student_hidden, weight_query, weight_key, doc_lengths):

    def one_group(inputs):
        teacher_queries, teacher_keys, hidden_rows, lengths = inputs
        student_queries = jnp.dot(hidden_rows, weight_query, preferred_element_type=jnp.float32).astype(jnp.bfloat16)
        student_keys = jnp.dot(hidden_rows, weight_key, preferred_element_type=jnp.float32).astype(jnp.bfloat16)
        bounds = jnp.cumsum(lengths).astype(jnp.int32)
        positions = jnp.arange(L, dtype=jnp.int32)
        documents = document_ids(positions, bounds)
        row_valid = documents < DOCS
        allowed = (documents[:, None] == documents[None, :]) & row_valid[:, None]
        valid_count = jnp.sum(lengths).astype(jnp.float32)
        coefficient = loss_scale / (H * valid_count)
        grad_queries, divergence_q = relation(teacher_queries, student_queries, allowed, row_valid, coefficient)
        grad_keys, divergence_k = relation(teacher_keys, student_keys, allowed, row_valid, coefficient)
        query_grad_b = grad_queries.astype(jnp.bfloat16)
        key_grad_b = grad_keys.astype(jnp.bfloat16)
        hidden_grad = (jnp.dot(query_grad_b, weight_query.T, preferred_element_type=jnp.float32) + jnp.dot(key_grad_b, weight_key.T, preferred_element_type=jnp.float32)).astype(jnp.bfloat16)
        both_grads = jnp.concatenate([query_grad_b, key_grad_b], axis=1)
        weight_terms = jnp.dot(hidden_rows.T, both_grads, preferred_element_type=jnp.float32)
        group_value = (divergence_q + divergence_k) / (H * valid_count)
        return (group_value, hidden_grad, weight_terms)
    losses, hidden_grads, weight_terms = lax.map(one_group, (teacher_query, teacher_key, student_hidden, doc_lengths))
    summed = lax.optimization_barrier(jnp.sum(weight_terms, axis=0))
    return (losses, hidden_grads, summed[:, :H * SDH], summed[:, H * SDH:])
```

```python
import math

import jax
import jax.numpy as jnp
from jax import lax
from jax.experimental import pallas as pl
from jax.experimental.pallas import tpu as pltpu
from jax.sharding import PartitionSpec as P

H = 16
TDH = 128
SDH = 48
DOCS = 8
ROWS = 128
SLOTS = 256
TAIL = 64
DS = 1536
TW = H * TDH
SW = H * SDH
LOSS_SCALE = 1048576.0
MASKED = -1e30
LOG2E = math.log2(math.e)
BF = jnp.bfloat16
F32 = jnp.float32
MESH = pl.DeviceIdType.MESH

PARTS = 3
ORDERS = (("y", "z", "x"), ("x", "y", "z"), ("z", "x", "y"))
EXTENT = {"xl": 2, "z": 4, "y": 4, "xh": 2}
UNIT = (48, 128)


def dims_of(axis):
    return ("xl", "xh") if axis == "x" else (axis,)


def stage_dims(order):
    dims = ("xl", "z", "y", "xh")
    found = [dims]
    for axis in order:
        dims = tuple(d for d in dims if d not in dims_of(axis))
        found.append(dims)
    return found


def extent(dims):
    return tuple(EXTENT[d] for d in dims)


def kernel(
    tq,
    tk,
    hid,
    wq,
    wk,
    lengths,
    out_loss,
    out_hidden,
    out_wq,
    out_wk,
    T,
    Ttail,
    Hd,
    Htail,
    HdT,
    Wown,
    Woth,
    S,
    E,
    G,
    Gb,
    GX,
    GT,
    Wb,
    agbuf,
    lossb,
    lossr,
    *rest,
):
    sums = rest[: 3 * PARTS + PARTS]
    recvs = rest[4 * PARTS : 4 * PARTS + 3 * PARTS]
    loc, tail_s, tail_r, rs_s, rs_r, ag_s, ag_r, loss_s, loss_r = rest[7 * PARTS :]

    dp = lax.axis_index("dp")
    ctx = lax.axis_index("ctx")
    y, xh = lax.div(dp, 2), lax.rem(dp, 2)
    core = lax.rem(ctx, 2)
    k = lax.div(ctx, 2)
    z, xl = lax.rem(k, 4), lax.div(k, 4)
    x = xh * 2 + xl
    coords = {"x": x, "y": y, "z": z}

    def device(x_, y_, z_, core_):
        return {"dp": y_ * 2 + lax.div(x_, 2), "ctx": (lax.rem(x_, 2) * 4 + z_) * 2 + core_}

    def along(axis, j):
        c = dict(coords)
        c[axis] = lax.rem(c[axis] + j, 4)
        return device(c["x"], c["y"], c["z"], core), c[axis]

    pair = {"dp": dp, "ctx": k * 2 + 1 - core}
    is0, is1 = core == 0, core == 1
    has_next, has_prev = k < 7, k > 0
    sends = jnp.logical_and(is1, has_next)

    mine = pl.ds(pl.multiple_of(core * ROWS, ROWS), ROWS)
    theirs = pl.ds(pl.multiple_of((1 - core) * ROWS, ROWS), ROWS)
    own_hidden = pltpu.make_async_copy(hid, Hd.at[mine], loc.at[0])
    own_hidden.start()

    def by_core(first, second, dst, sem):
        def go(src):
            def start():
                pltpu.make_async_copy(src, dst, sem).start()

            return start

        pl.when(is0)(go(first))
        pl.when(is1)(go(second))
        return pltpu.make_async_copy(first, dst, sem)

    w_own = by_core(wq, wk, Wown, loc.at[1])
    own_t = by_core(tq, tk, T.at[mine], loc.at[2])
    w_oth = by_core(wk, wq, Woth, loc.at[3])

    barrier = pltpu.get_barrier_semaphore()

    def hail(device_id):
        pl.semaphore_signal(barrier, inc=1, device_id=device_id, device_id_type=MESH)

    hail(pair)
    for j in range(1, 8):
        for c in range(2):
            hail({"dp": lax.rem(dp + j, 8), "ctx": k * 2 + c})
    for axis, j in (("x", 1), ("x", 3), ("z", 1), ("z", 2), ("z", 3)):
        hail(along(axis, j)[0])

    @pl.when(sends)
    def _():
        hail({"dp": dp, "ctx": k * 2 + 2})
        hail({"dp": dp, "ctx": k * 2 + 3})

    @pl.when(has_prev)
    def _():
        hail({"dp": dp, "ctx": k * 2 - 1})

    pl.semaphore_wait(
        barrier, 20 + jnp.where(sends, 2, 0) + jnp.where(has_prev, 1, 0)
    )

    pending = []

    def remote(src, dst, send_sem, recv_sem, device_id, cond=None):
        copy = pltpu.make_async_remote_copy(
            src_ref=src,
            dst_ref=dst,
            send_sem=send_sem,
            recv_sem=recv_sem,
            device_id=device_id,
            device_id_type=MESH,
        )
        if cond is None:
            copy.start()
        else:
            pl.when(cond)(copy.start)
        pending.append((copy, cond))
        return copy

    def arrived(dst, recv_sem, cond=None):
        copy = pltpu.make_async_remote_copy(
            src_ref=dst,
            dst_ref=dst,
            send_sem=recv_sem,
            recv_sem=recv_sem,
            device_id=pair,
            device_id_type=MESH,
        )
        if cond is None:
            copy.wait_recv()
        else:
            pl.when(cond)(copy.wait_recv)

    last = pl.ds(ROWS - TAIL, TAIL)
    remote(hid, Hd.at[mine], tail_s.at[0], tail_r.at[0], pair)
    for c in range(2):
        remote(
            hid.at[last], Htail, tail_s.at[1 + c], tail_r.at[1], {"dp": dp, "ctx": k * 2 + 2 + c}, sends
        )
    remote(tk, T.at[mine], tail_s.at[3], tail_r.at[2], pair, is0)
    remote(tq, T.at[mine], tail_s.at[3], tail_r.at[2], pair, is1)
    chunk = 512
    for q in range(TW // chunk):
        cols = pl.ds(q * chunk, chunk)
        for c, src in enumerate((tq, tk)):
            remote(
                src.at[last, cols],
                Ttail.at[:, cols],
                tail_s.at[4 + 2 * q + c],
                tail_r.at[3 + q],
                {"dp": dp, "ctx": k * 2 + 2 + c},
                sends,
            )

    start = jnp.int32(0)
    end = jnp.int32(0)
    count = jnp.int32(0)
    for i in range(DOCS):
        value = lengths[0, i]
        start = start + jnp.where(i < k, value, 0)
        end = end + jnp.where(i <= k, value, 0)
        count = count + value
    lo = end - SLOTS * k
    hi = start - SLOTS * (k - 1)
    mean_over = 1.0 / (H * jnp.full((1, 128), count, jnp.int32).astype(F32))
    coefficient = LOSS_SCALE * mean_over

    def slot(shape, first):
        return lax.broadcasted_iota(jnp.int32, shape, 0) + first

    def tail_mask(width):
        return slot((TAIL, width), SLOTS - TAIL) >= hi

    own_hidden.wait()
    w_own.wait()
    arrived(Hd.at[theirs], tail_r.at[0])
    for r in range(0, SLOTS, 128):
        S[r : r + 128, :] = jnp.dot(
            Hd[r : r + 128, :], Wown[...], preferred_element_type=F32
        ).astype(BF)
    arrived(Htail, tail_r.at[1], has_prev)
    tail_rows = slice(SLOTS - TAIL, SLOTS)
    projected = jnp.dot(Htail[...], Wown[...], preferred_element_type=F32).astype(BF)
    S[tail_rows, :] = jnp.where(tail_mask(SW), projected, S[tail_rows, :])
    Hd[tail_rows, :] = jnp.where(tail_mask(DS), Htail[...], Hd[tail_rows, :])
    for r in range(0, DS, 128):
        HdT[r : r + 128, :] = Hd[:, r : r + 128].T

    own_t.wait()
    arrived(T.at[theirs], tail_r.at[2])

    row_slot = lax.broadcasted_iota(jnp.int32, (SLOTS, 128), 0)
    row_lane = lax.broadcasted_iota(jnp.int32, (SLOTS, 128), 1)
    row_bad = jnp.logical_and(row_slot >= lo, row_slot < hi)
    row_bias = jnp.where(row_bad, MASKED, 0.0)
    bias_tile = jnp.where(row_lane == 0, row_bias, 0.0).astype(BF)
    one_tile = jnp.where(row_lane == 0, 1.0, 0.0).astype(BF)
    bias_all = row_bias.astype(BF)
    rate = []
    for cb in range(2):
        lane_slot = lax.broadcasted_iota(jnp.int32, (1, 128), 1) + 128 * cb
        good = jnp.logical_or(lane_slot < lo, lane_slot >= hi)
        rate.append(jnp.where(good, coefficient, 0.0))
    ct = LOG2E / math.sqrt(TDH)
    cs = LOG2E / math.sqrt(SDH)
    nt = (((1,), (1,)), ((), ()))

    G[...] = jnp.zeros_like(G)

    def probabilities(scores, factor, rate_here):
        high = jnp.max(scores, axis=0, keepdims=True)
        rel = (scores - high) * factor
        raw = jnp.exp2(rel)
        total = jnp.sum(raw, axis=0, keepdims=True)
        return rel, raw * (rate_here / total), jnp.log2(total)

    def head(h, loss):
        th = T[:, TDH * h : TDH * (h + 1)]
        lhs_t = jnp.concatenate([th, bias_tile], axis=1)
        rhs_t = jnp.concatenate([th, one_tile], axis=1)
        first = SDH * h
        a, b = first // 128, (first + SDH - 1) // 128
        width = (b - a + 1) * 128
        cols = slice(128 * a, 128 * a + width)
        st = S[:, cols]
        lane = lax.broadcasted_iota(jnp.int32, (SLOTS, width), 1) + 128 * a
        inside = jnp.logical_and(lane >= first, lane < first + SDH)
        spare = 128 * a if first > 128 * a else 128 * a + width - 1
        picked = jnp.where(inside, st, jnp.zeros_like(st))
        wide_bias = bias_all if width == 128 else jnp.concatenate([bias_all, bias_all], axis=1)
        lhs_s = jnp.where(lane == spare, wide_bias, picked)
        rhs_s = jnp.where(lane == spare, jnp.ones_like(st), st)
        for cb in range(2):
            block = slice(128 * cb, 128 * (cb + 1))
            t = lax.dot_general(lhs_t, rhs_t[block], nt, preferred_element_type=F32)
            s = lax.dot_general(lhs_s, rhs_s[block], nt, preferred_element_type=F32)
            rel_t, et, log_t = probabilities(t, ct, rate[cb])
            rel_s, es, log_s = probabilities(s, cs, rate[cb])
            E[:, block] = es - et
            loss = loss + jnp.sum(et * (rel_t - rel_s), axis=0, keepdims=True)
            loss = loss - rate[cb] * (log_t - log_s)
        e00, e01 = E[:128, :128], E[:128, 128:]
        e10, e11 = E[128:, :128], E[128:, 128:]
        w01 = e01 + e10.T
        Wb[:128, :128] = (e00 + e00.T).astype(BF)
        Wb[:128, 128:] = w01.astype(BF)
        Wb[128:, :128] = w01.T.astype(BF)
        Wb[128:, 128:] = (e11 + e11.T).astype(BF)
        G[:, cols] += jnp.dot(Wb[...], picked, preferred_element_type=F32)
        return loss

    def sub(ref, dims, axis, at):
        index = []
        for d in dims:
            if d not in dims_of(axis):
                index.append(slice(None))
            elif d == "xl":
                index.append(lax.rem(at, 2))
            elif d == "xh":
                index.append(lax.div(at, 2))
            else:
                index.append(at)
        return ref.at[tuple(index)]

    def send_stage(p, stage):
        order = ORDERS[p]
        dims = stage_dims(order)[stage]
        source = sums[4 * p + stage]
        for j in (2, 1, 3):
            peer, at = along(order[stage], j)
            n = (p * 3 + stage) * 3 + j - 1
            remote(
                sub(source, dims, order[stage], at),
                recvs[3 * p + stage].at[j - 1],
                rs_s.at[n],
                rs_r.at[n],
                peer,
            )

    def sum_stage(p, stage):
        order = ORDERS[p]
        dims = stage_dims(order)[stage]
        buf = recvs[3 * p + stage]
        total = sub(sums[4 * p + stage], dims, order[stage], coords[order[stage]])[...].astype(F32)
        for j in (1, 3, 2):
            arrived(buf.at[j - 1], rs_r.at[(p * 3 + stage) * 3 + j - 1])
            total = total + buf[j - 1].astype(F32)
        sums[4 * p + stage + 1][...] = total.astype(BF)

    def part_terms(p):
        cols = slice(256 * p, 256 * (p + 1))
        Gb[:, cols] = (G[:, cols] * (1.0 / math.sqrt(SDH))).astype(BF)
        for xl_ in range(2):
            terms = jnp.dot(
                HdT[768 * xl_ : 768 * (xl_ + 1), :], Gb[:, cols], preferred_element_type=F32
            ).astype(BF)
            for xh_ in range(2):
                sums[4 * p][xl_, :, :, xh_] = terms[:, 128 * xh_ : 128 * (xh_ + 1)].reshape(
                    (4, 4) + UNIT
                )
        send_stage(p, 0)

    yl = lax.rem(y, 2)
    goal = lax.div(y, 2)

    def send_final(p):
        block = sums[4 * p + 3]
        for j in range(8):
            dp_ = lax.rem(dp + j, 8)
            n = p * 8 + j
            cond = None if j else core != goal
            remote(
                block,
                agbuf.at[core, p, yl, xh],
                ag_s.at[n],
                ag_r.at[core, p, yl, xh],
                {"dp": dp_, "ctx": k * 2 + goal},
                cond,
            )

        @pl.when(core == goal)
        def _():
            agbuf[core, p, yl, xh] = block[...]

    loss = jnp.zeros((1, 128), F32)
    for h in range(H):
        if h % 4 == 0:
            cols = slice(TDH * h, TDH * (h + 4))
            arrived(Ttail.at[:, cols], tail_r.at[3 + h // 4], has_prev)
            T[tail_rows, cols] = jnp.where(tail_mask(TDH * 4), Ttail[:, cols], T[tail_rows, cols])
        loss = head(h, loss)
        if h == 5:
            part_terms(0)
        if h == 10:
            part_terms(1)
        if h == 15:
            part_terms(2)

    remote(Gb.at[theirs], GX, tail_s.at[12], tail_r.at[7], pair)
    remote(
        Gb.at[tail_rows],
        GT.at[core],
        tail_s.at[13],
        tail_r.at[8 + core],
        {"dp": dp, "ctx": k * 2 - 1},
        has_prev,
    )
    lossb[0] = jnp.broadcast_to(loss, (8, 128))
    for j in (1, 2, 3):
        remote(lossb.at[0], lossr.at[j - 1], loss_s.at[j - 1], loss_r.at[j - 1], along("z", j)[0])

    sum_stage(0, 0)
    send_stage(0, 1)
    sum_stage(1, 0)
    send_stage(1, 1)

    w_oth.wait()
    arrived(GX, tail_r.at[7])
    for c in range(2):
        arrived(GT.at[c], tail_r.at[8 + c], sends)
    rows = slice(ROWS - TAIL, ROWS)
    lent = slot((TAIL, SW), SLOTS - TAIL - ROWS + core * ROWS) >= lo
    zero = jnp.zeros((TAIL, SW), BF)
    keep = jnp.full((TAIL, SW), k, jnp.int32) < 7
    own_low = Gb[pl.ds(pl.multiple_of(core * ROWS, ROWS), ROWS - TAIL), :]
    own_high = Gb[pl.ds(pl.multiple_of(core * ROWS + ROWS - TAIL, TAIL), TAIL), :]
    own_high = jnp.where(lent, jnp.where(keep, GT[1], zero), own_high)
    GX[rows, :] = jnp.where(lent, jnp.where(keep, GT[0], zero), GX[rows, :])
    own_rows = jnp.concatenate([own_low, own_high], axis=0)
    for r in range(0, DS, 512):
        out_hidden[:, r : r + 512] = (
            lax.dot_general(own_rows, Wown[r : r + 512, :], nt, preferred_element_type=F32)
            + lax.dot_general(GX[...], Woth[r : r + 512, :], nt, preferred_element_type=F32)
        ).astype(BF)

    sum_stage(2, 0)
    send_stage(2, 1)
    for p in range(PARTS):
        sum_stage(p, 1)
        send_stage(p, 2)

    loss_total = lossb[0]
    for j in (1, 2, 3):
        arrived(lossr.at[j - 1], loss_r.at[j - 1])
        loss_total = loss_total + lossr[j - 1]
    lossb[1] = loss_total
    x_other = xh * 2 + 1 - xl
    remote(lossb.at[1], lossr.at[3], loss_s.at[3], loss_r.at[3], device(x_other, y, z, core))

    for p in range(PARTS):
        sum_stage(p, 2)
        send_final(p)

    arrived(lossr.at[3], loss_r.at[3])
    loss_total = loss_total + lossr[3]
    lossb[2] = loss_total
    remote(lossb.at[2], lossr.at[4], loss_s.at[4], loss_r.at[4], pair)
    arrived(lossr.at[4], loss_r.at[4])
    loss_total = loss_total + lossr[4]
    out_loss[...] = jnp.broadcast_to(
        jnp.sum(loss_total[:1], axis=1, keepdims=True) * (math.log(2.0) / LOSS_SCALE), (1, 128)
    )

    for p in range(PARTS):
        for r, out in enumerate((out_wq, out_wk)):
            for yl_ in range(2):
                for xh_ in range(2):
                    itself = jnp.logical_and(
                        jnp.logical_and(core == r, xh == xh_), y == 2 * core + yl_
                    )
                    arrived(
                        agbuf.at[r, p, yl_, xh_],
                        ag_r.at[r, p, yl_, xh_],
                        jnp.logical_not(itself),
                    )
                    at = 256 * p + 128 * xh_
                    out[48 * yl_ : 48 * (yl_ + 1), at : at + 128] = agbuf[r, p, yl_, xh_].astype(F32)

    for copy, cond in pending:
        if cond is None:
            copy.wait_send()
        else:
            pl.when(cond)(copy.wait_send)


def per_device(teacher_query, teacher_key, student_hidden, weight_query, weight_key, doc_lengths):
    scratch = [
        pltpu.VMEM((SLOTS, TW), BF),
        pltpu.VMEM((TAIL, TW), BF),
        pltpu.VMEM((SLOTS, DS), BF),
        pltpu.VMEM((TAIL, DS), BF),
        pltpu.VMEM((DS, SLOTS), BF),
        pltpu.VMEM((DS, SW), BF),
        pltpu.VMEM((DS, SW), BF),
        pltpu.VMEM((SLOTS, SW), BF),
        pltpu.VMEM((SLOTS, SLOTS), F32),
        pltpu.VMEM((SLOTS, SW), F32),
        pltpu.VMEM((SLOTS, SW), BF),
        pltpu.VMEM((ROWS, SW), BF),
        pltpu.VMEM((2, TAIL, SW), BF),
        pltpu.VMEM((SLOTS, SLOTS), BF),
        pltpu.VMEM((2, PARTS, 2, 2) + UNIT, BF),
        pltpu.VMEM((3, 8, 128), F32),
        pltpu.VMEM((5, 8, 128), F32),
    ]
    for order in ORDERS:
        for dims in stage_dims(order):
            scratch.append(pltpu.VMEM(extent(dims) + UNIT, BF))
    for order in ORDERS:
        for dims in stage_dims(order)[1:]:
            scratch.append(pltpu.VMEM((3,) + extent(dims) + UNIT, BF))
    dma = pltpu.SemaphoreType.DMA
    scratch += [
        dma((4,)),
        dma((14,)),
        dma((10,)),
        dma((27,)),
        dma((27,)),
        dma((24,)),
        dma((2, PARTS, 2, 2)),
        dma((5,)),
        dma((5,)),
    ]
    vmem = pl.BlockSpec(memory_space=pltpu.VMEM)
    anywhere = pl.BlockSpec(memory_space=pl.ANY)
    loss, hidden_grad, grad_wq, grad_wk = pl.pallas_call(
        kernel,
        out_shape=(
            jax.ShapeDtypeStruct((1, 128), F32),
            jax.ShapeDtypeStruct((ROWS, DS), BF),
            jax.ShapeDtypeStruct((96, SW), F32),
            jax.ShapeDtypeStruct((96, SW), F32),
        ),
        in_specs=[anywhere] * 5 + [pl.BlockSpec(memory_space=pltpu.SMEM)],
        out_specs=(vmem, vmem, vmem, vmem),
        scratch_shapes=scratch,
        compiler_params=pltpu.CompilerParams(
            collective_id=0, has_side_effects=True, vmem_limit_bytes=56 * 1024 * 1024
        ),
        name="relations",
    )(
        teacher_query[0],
        teacher_key[0],
        student_hidden[0],
        weight_query,
        weight_key,
        doc_lengths,
    )
    return loss[0, :1], hidden_grad[None], grad_wq, grad_wk


def solution(mesh):
    in_specs = (
        P("dp", "ctx", None),
        P("dp", "ctx", None),
        P("dp", "ctx", None),
        P(),
        P(),
        P("dp", None),
    )
    out_specs = (P("dp"), P("dp", "ctx", None), P("ctx", None), P("ctx", None))
    return jax.shard_map(
        per_device, mesh=mesh, in_specs=in_specs, out_specs=out_specs, check_vma=False
    )
```

```python
import math

import jax
import jax.numpy as jnp
from jax import lax
from jax.experimental import pallas as pl
from jax.experimental.pallas import tpu as pltpu
from jax.sharding import PartitionSpec as P

H = 16
TDH = 128
SDH = 48
DOCS = 8
ROWS = 128
SLOTS = 256
TAIL = 64
DS = 1536
TW = H * TDH
SW = H * SDH
LOSS_SCALE = 1048576.0
MASKED = -1e30
LOG2E = math.log2(math.e)
BF = jnp.bfloat16
F32 = jnp.float32
MESH = pl.DeviceIdType.MESH

CHUNKS = 3
PARTS = 3
XYZ, YZX, ZXY = ("x", "y", "z"), ("y", "z", "x"), ("z", "x", "y")
ORDERS = ((XYZ, YZX, XYZ), (YZX, XYZ, YZX), (ZXY, ZXY, XYZ))
READY = (5, 10, 15)
EXTENT = {"xl": 2, "z": 4, "y": 4, "xh": 2}
UNIT = (16, 128)
GROUPS_OF_HEADS = ((0, 4), (4, 8), (8, 12), (12, 14), (14, 16))


def dims_of(axis):
    return ("xl", "xh") if axis == "x" else (axis,)


def stage_dims(order):
    dims = ("xl", "z", "y", "xh")
    found = [dims]
    for axis in order:
        dims = tuple(d for d in dims if d not in dims_of(axis))
        found.append(dims)
    return found


def extent(dims):
    return tuple(EXTENT[d] for d in dims)


def kernel(
    tq,
    tk,
    hid,
    wq,
    wk,
    lengths,
    out_loss,
    out_hidden,
    out_terms,
    T,
    Ttail,
    Hd,
    Htail,
    HdT,
    Wown,
    Woth,
    S,
    E,
    G,
    Gb,
    GX,
    GT,
    Wb,
    agbuf,
    lossb,
    lossr,
    *rest,
):
    pieces = CHUNKS * PARTS
    sums = rest[: 3 * pieces]
    recvs = rest[3 * pieces : 6 * pieces]
    final, loc, tail_s, tail_r, rs_s, rs_r, ag_s, ag_r, loss_s, loss_r = rest[6 * pieces :]

    dp = lax.axis_index("dp")
    ctx = lax.axis_index("ctx")
    y, xh = lax.div(dp, 2), lax.rem(dp, 2)
    core = lax.rem(ctx, 2)
    k = lax.div(ctx, 2)
    z, xl = lax.rem(k, 4), lax.div(k, 4)
    x = xh * 2 + xl
    coords = {"x": x, "y": y, "z": z}

    def device(x_, y_, z_, core_):
        return {"dp": y_ * 2 + lax.div(x_, 2), "ctx": (lax.rem(x_, 2) * 4 + z_) * 2 + core_}

    def along(axis, j):
        c = dict(coords)
        c[axis] = lax.rem(c[axis] + j, 4)
        return device(c["x"], c["y"], c["z"], core), c[axis]

    pair = {"dp": dp, "ctx": k * 2 + 1 - core}
    is0, is1 = core == 0, core == 1
    has_next, has_prev = k < 7, k > 0
    sends = jnp.logical_and(is1, has_next)

    mine = pl.ds(pl.multiple_of(core * ROWS, ROWS), ROWS)
    theirs = pl.ds(pl.multiple_of((1 - core) * ROWS, ROWS), ROWS)
    own_hidden = pltpu.make_async_copy(hid, Hd.at[mine], loc.at[0])
    own_hidden.start()

    def by_core(first, second, dst, sem):
        def go(src):
            def start():
                pltpu.make_async_copy(src, dst, sem).start()

            return start

        pl.when(is0)(go(first))
        pl.when(is1)(go(second))
        return pltpu.make_async_copy(first, dst, sem)

    w_own = by_core(wq, wk, Wown, loc.at[1])
    own_t = by_core(tq, tk, T.at[mine], loc.at[2])
    w_oth = by_core(wk, wq, Woth, loc.at[3])

    barrier = pltpu.get_barrier_semaphore()

    def hail(device_id):
        pl.semaphore_signal(barrier, inc=1, device_id=device_id, device_id_type=MESH)

    hail(pair)
    for j in range(1, 8):
        for c in range(2):
            hail({"dp": lax.rem(dp + j, 8), "ctx": k * 2 + c})
    for axis, j in (("x", 1), ("x", 3), ("z", 1), ("z", 2), ("z", 3)):
        hail(along(axis, j)[0])

    @pl.when(sends)
    def _():
        hail({"dp": dp, "ctx": k * 2 + 2})
        hail({"dp": dp, "ctx": k * 2 + 3})

    @pl.when(has_prev)
    def _():
        hail({"dp": dp, "ctx": k * 2 - 1})

    pl.semaphore_wait(
        barrier, 20 + jnp.where(sends, 2, 0) + jnp.where(has_prev, 1, 0)
    )

    pending = []

    def remote(src, dst, send_sem, recv_sem, device_id, cond=None):
        copy = pltpu.make_async_remote_copy(
            src_ref=src,
            dst_ref=dst,
            send_sem=send_sem,
            recv_sem=recv_sem,
            device_id=device_id,
            device_id_type=MESH,
        )
        if cond is None:
            copy.start()
        else:
            pl.when(cond)(copy.start)
        pending.append((copy, cond))
        return copy

    def arrived(dst, recv_sem, cond=None):
        copy = pltpu.make_async_remote_copy(
            src_ref=dst,
            dst_ref=dst,
            send_sem=recv_sem,
            recv_sem=recv_sem,
            device_id=pair,
            device_id_type=MESH,
        )
        if cond is None:
            copy.wait_recv()
        else:
            pl.when(cond)(copy.wait_recv)

    last = pl.ds(ROWS - TAIL, TAIL)
    half = DS // 2
    remote(hid, Hd.at[mine], tail_s.at[0], tail_r.at[0], pair)
    for c in range(2):
        cols = pl.ds(c * half, half)
        remote(
            hid.at[last, cols],
            Htail.at[:, cols],
            tail_s.at[1 + c],
            tail_r.at[1],
            {"dp": dp, "ctx": k * 2 + 2 + c},
            sends,
        )
    remote(tk, T.at[mine], tail_s.at[3], tail_r.at[2], pair, is0)
    remote(tq, T.at[mine], tail_s.at[3], tail_r.at[2], pair, is1)
    for q, (h0, h1) in enumerate(GROUPS_OF_HEADS):
        cols = pl.ds(TDH * h0, TDH * (h1 - h0))
        for c, src in enumerate((tq, tk)):
            remote(
                src.at[last, cols],
                Ttail.at[:, cols],
                tail_s.at[4 + 2 * q + c],
                tail_r.at[3 + q],
                {"dp": dp, "ctx": k * 2 + 2 + c},
                sends,
            )

    start = jnp.int32(0)
    end = jnp.int32(0)
    count = jnp.int32(0)
    for i in range(DOCS):
        value = lengths[0, i]
        start = start + jnp.where(i < k, value, 0)
        end = end + jnp.where(i <= k, value, 0)
        count = count + value
    lo = end - SLOTS * k
    hi = start - SLOTS * (k - 1)
    mean_over = 1.0 / (H * jnp.full((1, 128), count, jnp.int32).astype(F32))
    coefficient = LOSS_SCALE * mean_over

    def slot(shape, first):
        return lax.broadcasted_iota(jnp.int32, shape, 0) + first

    def tail_mask(width):
        return slot((TAIL, width), SLOTS - TAIL) >= hi

    own_hidden.wait()
    w_own.wait()
    arrived(Hd.at[theirs], tail_r.at[0])
    for r in range(0, SLOTS, 128):
        S[r : r + 128, :] = jnp.dot(
            Hd[r : r + 128, :], Wown[...], preferred_element_type=F32
        ).astype(BF)
    my_half = Htail.at[:, pl.ds(pl.multiple_of(core * half, half), half)]
    arrived(my_half, tail_r.at[1], has_prev)
    remote(my_half, my_half, tail_s.at[14], tail_r.at[11], pair, has_prev)
    arrived(my_half, tail_r.at[11], has_prev)
    tail_rows = slice(SLOTS - TAIL, SLOTS)
    projected = jnp.dot(Htail[...], Wown[...], preferred_element_type=F32).astype(BF)
    S[tail_rows, :] = jnp.where(tail_mask(SW), projected, S[tail_rows, :])
    Hd[tail_rows, :] = jnp.where(tail_mask(DS), Htail[...], Hd[tail_rows, :])
    for r in range(0, DS, 128):
        HdT[r : r + 128, :] = Hd[:, r : r + 128].T

    own_t.wait()
    arrived(T.at[theirs], tail_r.at[2])

    row_slot = lax.broadcasted_iota(jnp.int32, (SLOTS, 128), 0)
    row_lane = lax.broadcasted_iota(jnp.int32, (SLOTS, 128), 1)
    row_bad = jnp.logical_and(row_slot >= lo, row_slot < hi)
    row_bias = jnp.where(row_bad, MASKED, 0.0)
    bias_tile = jnp.where(row_lane == 0, row_bias, 0.0).astype(BF)
    one_tile = jnp.where(row_lane == 0, 1.0, 0.0).astype(BF)
    bias_all = row_bias.astype(BF)
    rate = []
    for cb in range(2):
        lane_slot = lax.broadcasted_iota(jnp.int32, (1, 128), 1) + 128 * cb
        good = jnp.logical_or(lane_slot < lo, lane_slot >= hi)
        rate.append(jnp.where(good, coefficient, 0.0))
    ct = LOG2E / math.sqrt(TDH)
    cs = LOG2E / math.sqrt(SDH)
    nt = (((1,), (1,)), ((), ()))

    G[...] = jnp.zeros_like(G)

    def probabilities(scores, factor, rate_here):
        high = jnp.max(scores, axis=0, keepdims=True)
        rel = (scores - high) * factor
        raw = jnp.exp2(rel)
        total = jnp.sum(raw, axis=0, keepdims=True)
        return rel, raw * (rate_here / total), jnp.log2(total)

    def head(h, loss):
        th = T[:, TDH * h : TDH * (h + 1)]
        lhs_t = jnp.concatenate([th, bias_tile], axis=1)
        rhs_t = jnp.concatenate([th, one_tile], axis=1)
        first = SDH * h
        a, b = first // 128, (first + SDH - 1) // 128
        width = (b - a + 1) * 128
        cols = slice(128 * a, 128 * a + width)
        st = S[:, cols]
        lane = lax.broadcasted_iota(jnp.int32, (SLOTS, width), 1) + 128 * a
        inside = jnp.logical_and(lane >= first, lane < first + SDH)
        spare = 128 * a if first > 128 * a else 128 * a + width - 1
        picked = jnp.where(inside, st, jnp.zeros_like(st))
        wide_bias = bias_all if width == 128 else jnp.concatenate([bias_all, bias_all], axis=1)
        lhs_s = jnp.where(lane == spare, wide_bias, picked)
        rhs_s = jnp.where(lane == spare, jnp.ones_like(st), st)
        for cb in range(2):
            block = slice(128 * cb, 128 * (cb + 1))
            t = lax.dot_general(lhs_t, rhs_t[block], nt, preferred_element_type=F32)
            s = lax.dot_general(lhs_s, rhs_s[block], nt, preferred_element_type=F32)
            rel_t, et, log_t = probabilities(t, ct, rate[cb])
            rel_s, es, log_s = probabilities(s, cs, rate[cb])
            E[:, block] = es - et
            loss = loss + jnp.sum(et * (rel_t - rel_s), axis=0, keepdims=True)
            loss = loss - rate[cb] * (log_t - log_s)
        e00, e01 = E[:128, :128], E[:128, 128:]
        e10, e11 = E[128:, :128], E[128:, 128:]
        w01 = e01 + e10.T
        Wb[:128, :128] = (e00 + e00.T).astype(BF)
        Wb[:128, 128:] = w01.astype(BF)
        Wb[128:, :128] = w01.T.astype(BF)
        Wb[128:, 128:] = (e11 + e11.T).astype(BF)
        G[:, cols] += jnp.dot(Wb[...], picked, preferred_element_type=F32)
        return loss

    def sub(ref, dims, axis, at):
        index = []
        for d in dims:
            if d not in dims_of(axis):
                index.append(slice(None))
            elif d == "xl":
                index.append(lax.rem(at, 2))
            elif d == "xh":
                index.append(lax.div(at, 2))
            else:
                index.append(at)
        return ref.at[tuple(index)]

    def send_stage(c, p, stage):
        order = ORDERS[c][p]
        dims = stage_dims(order)[stage]
        piece = c * PARTS + p
        source = sums[3 * piece + stage]
        for j in (2, 1, 3):
            peer, at = along(order[stage], j)
            n = (piece * 3 + stage) * 3 + j - 1
            remote(
                sub(source, dims, order[stage], at),
                recvs[3 * piece + stage].at[j - 1],
                rs_s.at[n],
                rs_r.at[n],
                peer,
            )

    def sum_stage(c, p, stage):
        order = ORDERS[c][p]
        dims = stage_dims(order)[stage]
        piece = c * PARTS + p
        buf = recvs[3 * piece + stage]
        total = sub(sums[3 * piece + stage], dims, order[stage], coords[order[stage]])[...].astype(F32)
        for j in (1, 3, 2):
            arrived(buf.at[j - 1], rs_r.at[(piece * 3 + stage) * 3 + j - 1])
            total = total + buf[j - 1].astype(F32)
        if stage < 2:
            sums[3 * piece + stage + 1][...] = total.astype(BF)
        else:
            final[c, 16 * p : 16 * (p + 1)] = total.astype(BF)

    def advance(c, stage):
        for p in range(PARTS):
            sum_stage(c, p, stage)
            if stage < 2:
                send_stage(c, p, stage + 1)
        if stage == 2:
            send_final(c)

    def chunk_terms(c):
        cols = slice(256 * c, 256 * (c + 1))
        Gb[:, cols] = (G[:, cols] * (1.0 / math.sqrt(SDH))).astype(BF)
        for xl_ in range(2):
            terms = (
                jnp.dot(HdT[768 * xl_ : 768 * (xl_ + 1), :], Gb[:, cols], preferred_element_type=F32)
                .astype(BF)
                .reshape(4, 4, PARTS, 16, 256)
            )
            for p in range(PARTS):
                for xh_ in range(2):
                    sums[3 * (c * PARTS + p)][xl_, :, :, xh_] = terms[
                        :, :, p, :, 128 * xh_ : 128 * (xh_ + 1)
                    ]
        for p in range(PARTS):
            send_stage(c, p, 0)

    yl = lax.rem(y, 2)
    goal = lax.div(y, 2)

    def send_final(c):
        for j in range(8):
            remote(
                final.at[c],
                agbuf.at[core, c, yl, xh],
                ag_s.at[c * 8 + j],
                ag_r.at[core, c, yl, xh],
                {"dp": lax.rem(dp + j, 8), "ctx": k * 2 + goal},
                None if j else core != goal,
            )

        @pl.when(core == goal)
        def _():
            agbuf[core, c, yl, xh] = final[c]

    loss = jnp.zeros((1, 128), F32)
    for q, (h0, h1) in enumerate(GROUPS_OF_HEADS):
        cols = slice(TDH * h0, TDH * h1)
        arrived(Ttail.at[:, cols], tail_r.at[3 + q], has_prev)
        T[tail_rows, cols] = jnp.where(
            tail_mask(TDH * (h1 - h0)), Ttail[:, cols], T[tail_rows, cols]
        )
        for h in range(h0, h1):
            loss = head(h, loss)
            if h in READY:
                chunk_terms(READY.index(h))

    remote(Gb.at[theirs], GX, tail_s.at[15], tail_r.at[8], pair)
    remote(
        Gb.at[tail_rows],
        GT.at[core],
        tail_s.at[16],
        tail_r.at[9 + core],
        {"dp": dp, "ctx": k * 2 - 1},
        has_prev,
    )
    lossb[0] = jnp.broadcast_to(loss, (8, 128))
    for j in (1, 2, 3):
        remote(lossb.at[0], lossr.at[j - 1], loss_s.at[j - 1], loss_r.at[j - 1], along("z", j)[0])

    advance(0, 0)

    w_oth.wait()
    arrived(GX, tail_r.at[8])
    for c in range(2):
        arrived(GT.at[c], tail_r.at[9 + c], sends)
    rows = slice(ROWS - TAIL, ROWS)
    lent = slot((TAIL, SW), SLOTS - TAIL - ROWS + core * ROWS) >= lo
    zero = jnp.zeros((TAIL, SW), BF)
    keep = jnp.full((TAIL, SW), k, jnp.int32) < 7
    own_low = Gb[pl.ds(pl.multiple_of(core * ROWS, ROWS), ROWS - TAIL), :]
    own_high = Gb[pl.ds(pl.multiple_of(core * ROWS + ROWS - TAIL, TAIL), TAIL), :]
    own_high = jnp.where(lent, jnp.where(keep, GT[1], zero), own_high)
    GX[rows, :] = jnp.where(lent, jnp.where(keep, GT[0], zero), GX[rows, :])
    own_rows = jnp.concatenate([own_low, own_high], axis=0)
    for r in range(0, DS, 512):
        out_hidden[:, r : r + 512] = (
            lax.dot_general(own_rows, Wown[r : r + 512, :], nt, preferred_element_type=F32)
            + lax.dot_general(GX[...], Woth[r : r + 512, :], nt, preferred_element_type=F32)
        ).astype(BF)

    advance(1, 0)
    advance(0, 1)
    advance(2, 0)
    advance(1, 1)
    advance(0, 2)

    loss_total = lossb[0]
    for j in (1, 2, 3):
        arrived(lossr.at[j - 1], loss_r.at[j - 1])
        loss_total = loss_total + lossr[j - 1]
    lossb[1] = loss_total
    x_other = xh * 2 + 1 - xl
    remote(lossb.at[1], lossr.at[3], loss_s.at[3], loss_r.at[3], device(x_other, y, z, core))

    advance(2, 1)
    advance(1, 2)
    advance(2, 2)

    arrived(lossr.at[3], loss_r.at[3])
    loss_total = loss_total + lossr[3]
    lossb[2] = loss_total
    remote(lossb.at[2], lossr.at[4], loss_s.at[4], loss_r.at[4], pair)
    arrived(lossr.at[4], loss_r.at[4])
    loss_total = loss_total + lossr[4]
    out_loss[...] = jnp.broadcast_to(
        jnp.sum(loss_total[:1], axis=1, keepdims=True) * (math.log(2.0) / LOSS_SCALE), (1, 128)
    )

    for c in range(CHUNKS):
        for r in range(2):
            for yl_ in range(2):
                for xh_ in range(2):
                    itself = jnp.logical_and(
                        jnp.logical_and(core == r, xh == xh_), y == 2 * core + yl_
                    )
                    arrived(
                        agbuf.at[r, c, yl_, xh_],
                        ag_r.at[r, c, yl_, xh_],
                        jnp.logical_not(itself),
                    )
    out_terms[...] = agbuf[...]

    for copy, cond in pending:
        if cond is None:
            copy.wait_send()
        else:
            pl.when(cond)(copy.wait_send)


def finish(loss, hidden_grad, terms, out_loss, out_hidden, out_wq, out_wk):
    out_loss[0] = loss[0, 0]
    out_hidden[...] = hidden_grad[...]
    for r, out in enumerate((out_wq, out_wk)):
        for c in range(CHUNKS):
            for yl in range(2):
                for xh in range(2):
                    at = 256 * c + 128 * xh
                    out[48 * yl : 48 * (yl + 1), at : at + 128] = terms[r, c, yl, xh].astype(F32)


def per_device(teacher_query, teacher_key, student_hidden, weight_query, weight_key, doc_lengths):
    scratch = [
        pltpu.VMEM((SLOTS, TW), BF),
        pltpu.VMEM((TAIL, TW), BF),
        pltpu.VMEM((SLOTS, DS), BF),
        pltpu.VMEM((TAIL, DS), BF),
        pltpu.VMEM((DS, SLOTS), BF),
        pltpu.VMEM((DS, SW), BF),
        pltpu.VMEM((DS, SW), BF),
        pltpu.VMEM((SLOTS, SW), BF),
        pltpu.VMEM((SLOTS, SLOTS), F32),
        pltpu.VMEM((SLOTS, SW), F32),
        pltpu.VMEM((SLOTS, SW), BF),
        pltpu.VMEM((ROWS, SW), BF),
        pltpu.VMEM((2, TAIL, SW), BF),
        pltpu.VMEM((SLOTS, SLOTS), BF),
        pltpu.VMEM((2, CHUNKS, 2, 2, 48, 128), BF),
        pltpu.VMEM((3, 8, 128), F32),
        pltpu.VMEM((5, 8, 128), F32),
    ]
    for orders in ORDERS:
        for order in orders:
            for dims in stage_dims(order)[:3]:
                scratch.append(pltpu.VMEM(extent(dims) + UNIT, BF))
    for orders in ORDERS:
        for order in orders:
            for dims in stage_dims(order)[1:]:
                scratch.append(pltpu.VMEM((3,) + extent(dims) + UNIT, BF))
    scratch.append(pltpu.VMEM((CHUNKS, 48, 128), BF))
    dma = pltpu.SemaphoreType.DMA
    scratch += [
        dma((4,)),
        dma((17,)),
        dma((12,)),
        dma((81,)),
        dma((81,)),
        dma((24,)),
        dma((2, CHUNKS, 2, 2)),
        dma((5,)),
        dma((5,)),
    ]
    vmem = pl.BlockSpec(memory_space=pltpu.VMEM)
    anywhere = pl.BlockSpec(memory_space=pl.ANY)
    loss, hidden_grad, terms = pl.pallas_call(
        kernel,
        out_shape=(
            jax.ShapeDtypeStruct((1, 128), F32),
            jax.ShapeDtypeStruct((ROWS, DS), BF),
            jax.ShapeDtypeStruct((2, CHUNKS, 2, 2, 48, 128), BF),
        ),
        in_specs=[anywhere] * 5 + [pl.BlockSpec(memory_space=pltpu.SMEM)],
        out_specs=(vmem, vmem, vmem),
        scratch_shapes=scratch,
        compiler_params=pltpu.CompilerParams(
            collective_id=0, has_side_effects=True, vmem_limit_bytes=56 * 1024 * 1024
        ),
        name="relations",
    )(
        teacher_query[0],
        teacher_key[0],
        student_hidden[0],
        weight_query,
        weight_key,
        doc_lengths,
    )
    smem = pl.BlockSpec(memory_space=pltpu.SMEM)
    loss, hidden_grad, grad_wq, grad_wk = pl.pallas_call(
        finish,
        out_shape=(
            jax.ShapeDtypeStruct((1,), F32),
            jax.ShapeDtypeStruct((ROWS, DS), BF),
            jax.ShapeDtypeStruct((96, SW), F32),
            jax.ShapeDtypeStruct((96, SW), F32),
        ),
        in_specs=[smem, vmem, vmem],
        out_specs=(smem, vmem, vmem, vmem),
        name="finish",
    )(loss, hidden_grad, terms)
    return loss, hidden_grad[None], grad_wq, grad_wk


def solution(mesh):
    in_specs = (
        P("dp", "ctx", None),
        P("dp", "ctx", None),
        P("dp", "ctx", None),
        P(),
        P(),
        P("dp", None),
    )
    out_specs = (P("dp"), P("dp", "ctx", None), P("ctx", None), P("ctx", None))
    return jax.shard_map(
        per_device, mesh=mesh, in_specs=in_specs, out_specs=out_specs, check_vma=False
    )
```

```python
import math

import jax
import jax.numpy as jnp
from jax import lax
from jax.experimental import pallas as pl
from jax.experimental.pallas import tpu as pltpu
from jax.sharding import PartitionSpec as P

H = 16
TDH = 128
SDH = 48
DOCS = 8
ROWS = 128
SLOTS = 256
TAIL = 64
DS = 1536
TW = H * TDH
SW = H * SDH
LOSS_SCALE = 1048576.0
MASKED = -1e30
LOG2E = math.log2(math.e)
BF = jnp.bfloat16
F32 = jnp.float32
MESH = pl.DeviceIdType.MESH

CHUNKS = 3
PARTS = 3
FIRST_AXIS = (("x", "y", "x"), ("y", "x", "y"), ("z", "z", "x"))
READY = (5, 10, 15)
EXTENT = {"xl": 2, "z": 4, "y": 4, "xh": 2}
UNIT = (16, 128)
GROUPS_OF_HEADS = ((0, 4), (4, 8), (8, 12), (12, 14), (14, 16))


def dims_of(axis):
    return ("xl", "xh") if axis == "x" else (axis,)


def left_after(axis):
    return tuple(d for d in ("xl", "z", "y", "xh") if d not in dims_of(axis))


def extent(dims):
    return tuple(EXTENT[d] for d in dims)


def kernel(
    tq,
    tk,
    hid,
    wq,
    wk,
    lengths,
    out_loss,
    out_hidden,
    out_terms,
    T,
    Ttail,
    Hd,
    Htail,
    HdT,
    Wown,
    Woth,
    S,
    X,
    E,
    G,
    Gb,
    GX,
    GT,
    Wb,
    agbuf,
    final,
    lossb,
    lossr,
    spare,
    *rest,
):
    pieces = CHUNKS * PARTS
    terms_of, halved, in_line, in_plane = (
        rest[i * pieces : (i + 1) * pieces] for i in range(4)
    )
    loc, tail_s, tail_r, rs_s, rs_r, ag_s, ag_r, loss_s, loss_r = rest[4 * pieces :]

    dp = lax.axis_index("dp")
    ctx = lax.axis_index("ctx")
    y, xh = lax.div(dp, 2), lax.rem(dp, 2)
    core = lax.rem(ctx, 2)
    k = lax.div(ctx, 2)
    z, xl = lax.rem(k, 4), lax.div(k, 4)
    x = xh * 2 + xl
    coords = {"x": x, "y": y, "z": z}

    def device(x_, y_, z_, core_):
        return {"dp": y_ * 2 + lax.div(x_, 2), "ctx": (lax.rem(x_, 2) * 4 + z_) * 2 + core_}

    def along(axis, j):
        c = dict(coords)
        c[axis] = lax.rem(c[axis] + j, 4)
        return device(c["x"], c["y"], c["z"], core), c[axis]

    pair = {"dp": dp, "ctx": k * 2 + 1 - core}
    is0, is1 = core == 0, core == 1
    has_next, has_prev = k < 7, k > 0
    sends = jnp.logical_and(is1, has_next)

    mine = pl.ds(pl.multiple_of(core * ROWS, ROWS), ROWS)
    theirs = pl.ds(pl.multiple_of((1 - core) * ROWS, ROWS), ROWS)
    own_hidden = pltpu.make_async_copy(hid, Hd.at[mine], loc.at[0])
    own_hidden.start()

    def by_core(first, second, dst, sem):
        def go(src):
            def start():
                pltpu.make_async_copy(src, dst, sem).start()

            return start

        pl.when(is0)(go(first))
        pl.when(is1)(go(second))
        return pltpu.make_async_copy(first, dst, sem)

    w_own = by_core(wq, wk, Wown, loc.at[1])
    own_t = by_core(tq, tk, T.at[mine], loc.at[2])
    w_oth = by_core(wk, wq, Woth, loc.at[3])

    barrier = pltpu.get_barrier_semaphore()

    def hail(device_id):
        pl.semaphore_signal(barrier, inc=1, device_id=device_id, device_id_type=MESH)

    hail(pair)
    for axis in ("x", "y", "z"):
        for j in (1, 2, 3):
            hail(along(axis, j)[0])

    @pl.when(sends)
    def _():
        hail({"dp": dp, "ctx": k * 2 + 2})
        hail({"dp": dp, "ctx": k * 2 + 3})

    @pl.when(has_prev)
    def _():
        hail({"dp": dp, "ctx": k * 2 - 1})

    pl.semaphore_wait(
        barrier, 10 + jnp.where(sends, 2, 0) + jnp.where(has_prev, 1, 0)
    )

    pending = []

    def copy_of(src, dst, send_sem, recv_sem, device_id):
        return pltpu.make_async_remote_copy(
            src_ref=src,
            dst_ref=dst,
            send_sem=send_sem,
            recv_sem=recv_sem,
            device_id=device_id,
            device_id_type=MESH,
        )

    def when(cond, act):
        if cond is None:
            act()
        else:
            pl.when(cond)(act)

    def remote(src, dst, send_sem, recv_sem, device_id, cond=None):
        when(cond, copy_of(src, dst, send_sem, recv_sem, device_id).start)

    def sent(like, send_sem, cond=None):
        pending.append((copy_of(like, like, send_sem, send_sem, pair), cond))

    def arrived(dst, recv_sem, cond=None):
        when(cond, copy_of(dst, dst, recv_sem, recv_sem, pair).wait_recv)

    last = pl.ds(ROWS - TAIL, TAIL)
    half = DS // 2
    remote(hid, Hd.at[mine], tail_s.at[0], tail_r.at[0], pair)
    sent(Hd.at[mine], tail_s.at[0])
    for c in range(2):
        cols = pl.ds(c * half, half)
        remote(
            hid.at[last, cols],
            Htail.at[:, cols],
            tail_s.at[1],
            tail_r.at[1],
            {"dp": dp, "ctx": k * 2 + 2 + c},
            sends,
        )
    sent(Htail, tail_s.at[1], sends)
    remote(tk, T.at[mine], tail_s.at[2], tail_r.at[2], pair, is0)
    remote(tq, T.at[mine], tail_s.at[2], tail_r.at[2], pair, is1)
    sent(T.at[mine], tail_s.at[2])
    for q, (h0, h1) in enumerate(GROUPS_OF_HEADS):
        cols = pl.ds(TDH * h0, TDH * (h1 - h0))
        for c, src in enumerate((tq, tk)):
            remote(
                src.at[last, cols],
                Ttail.at[:, cols],
                tail_s.at[3],
                tail_r.at[3 + q],
                {"dp": dp, "ctx": k * 2 + 2 + c},
                sends,
            )
    sent(T.at[mine], tail_s.at[3], sends)

    start = jnp.int32(0)
    end = jnp.int32(0)
    count = jnp.int32(0)
    for i in range(DOCS):
        value = lengths[0, i]
        start = start + jnp.where(i < k, value, 0)
        end = end + jnp.where(i <= k, value, 0)
        count = count + value
    lo = end - SLOTS * k
    hi = start - SLOTS * (k - 1)
    mean_over = 1.0 / (H * jnp.full((1, 128), count, jnp.int32).astype(F32))
    coefficient = LOSS_SCALE * mean_over

    def slot(shape, first):
        return lax.broadcasted_iota(jnp.int32, shape, 0) + first

    def tail_mask(width):
        return slot((TAIL, width), SLOTS - TAIL) >= hi

    own_hidden.wait()
    w_own.wait()
    arrived(Hd.at[theirs], tail_r.at[0])
    for r in range(0, SLOTS, 128):
        S[r : r + 128, :] = jnp.dot(
            Hd[r : r + 128, :], Wown[...], preferred_element_type=F32
        ).astype(BF)
    my_half = Htail.at[:, pl.ds(pl.multiple_of(core * half, half), half)]
    arrived(my_half, tail_r.at[1], has_prev)
    remote(my_half, my_half, tail_s.at[4], tail_r.at[11], pair, has_prev)
    sent(my_half, tail_s.at[4], has_prev)
    other_half = Htail.at[:, pl.ds(pl.multiple_of((1 - core) * half, half), half)]
    arrived(other_half, tail_r.at[11], has_prev)
    tail_rows = slice(SLOTS - TAIL, SLOTS)
    projected = jnp.dot(Htail[...], Wown[...], preferred_element_type=F32).astype(BF)
    S[tail_rows, :] = jnp.where(tail_mask(SW), projected, S[tail_rows, :])
    Hd[tail_rows, :] = jnp.where(tail_mask(DS), Htail[...], Hd[tail_rows, :])
    for r in range(0, DS, 128):
        HdT[r : r + 128, :] = Hd[:, r : r + 128].T

    own_t.wait()
    arrived(T.at[theirs], tail_r.at[2])

    row_slot = lax.broadcasted_iota(jnp.int32, (SLOTS, 128), 0)
    row_lane = lax.broadcasted_iota(jnp.int32, (SLOTS, 128), 1)
    row_bad = jnp.logical_and(row_slot >= lo, row_slot < hi)
    row_bias = jnp.where(row_bad, MASKED, 0.0)
    bias_tile = jnp.where(row_lane == 0, row_bias, 0.0).astype(BF)
    one_tile = jnp.where(row_lane == 0, 1.0, 0.0).astype(BF)
    bias_all = row_bias.astype(BF)
    rate = []
    for cb in range(2):
        lane_slot = lax.broadcasted_iota(jnp.int32, (1, 128), 1) + 128 * cb
        good = jnp.logical_or(lane_slot < lo, lane_slot >= hi)
        rate.append(jnp.where(good, coefficient, 0.0))
    ct = LOG2E / math.sqrt(TDH)
    cs = LOG2E / math.sqrt(SDH)
    nt = (((1,), (1,)), ((), ()))

    G[...] = jnp.zeros_like(G)

    def probabilities(scores, factor, rate_here):
        high = jnp.max(scores, axis=0, keepdims=True)
        rel = (scores - high) * factor
        raw = jnp.exp2(rel)
        total = jnp.sum(raw, axis=0, keepdims=True)
        return rel, raw * (rate_here / total), jnp.log2(total)

    def student_tiles(h):
        first = SDH * h
        a, b = first // 128, (first + SDH - 1) // 128
        width = (b - a + 1) * 128
        cols = slice(128 * a, 128 * a + width)
        st = S[:, cols]
        lane = lax.broadcasted_iota(jnp.int32, (SLOTS, width), 1) + 128 * a
        inside = jnp.logical_and(lane >= first, lane < first + SDH)
        free = 128 * a if first > 128 * a else 128 * a + width - 1
        return cols, st, jnp.where(inside, st, jnp.zeros_like(st)), lane == free

    def scores(h):
        th = T[:, TDH * h : TDH * (h + 1)]
        X[h % 2] = lax.dot_general(
            jnp.concatenate([th, bias_tile], axis=1),
            jnp.concatenate([th, one_tile], axis=1),
            nt,
            preferred_element_type=F32,
        )
        _, st, picked, free = student_tiles(h)
        bias = jnp.concatenate([bias_all] * (st.shape[1] // 128), axis=1)
        X[2 + h % 2] = lax.dot_general(
            jnp.where(free, bias, picked),
            jnp.where(free, jnp.ones_like(st), st),
            nt,
            preferred_element_type=F32,
        )

    def softmaxes(h, loss):
        for cb in range(2):
            block = slice(128 * cb, 128 * (cb + 1))
            rel_t, et, log_t = probabilities(X[h % 2, :, block], ct, rate[cb])
            rel_s, es, log_s = probabilities(X[2 + h % 2, :, block], cs, rate[cb])
            E[h % 2, :, block] = es - et
            loss = loss + jnp.sum(et * (rel_t - rel_s), axis=0, keepdims=True)
            loss = loss - rate[cb] * (log_t - log_s)
        return loss

    def weigh(h):
        e, w = E.at[h % 2], Wb.at[h % 2]
        cross = e[:128, 128:] + e[128:, :128].T
        for b in range(2):
            block = slice(128 * b, 128 * (b + 1))
            square = e[block, block]
            w[block, block] = (square + square.T).astype(BF)
        w[:128, 128:] = cross.astype(BF)
        w[128:, :128] = cross.T.astype(BF)

    def gradient(h):
        cols, _, picked, _ = student_tiles(h)
        G[:, cols] += jnp.dot(Wb[h % 2], picked, preferred_element_type=F32)

    def at_peer(dims, place):
        index = []
        for d in dims:
            if d in ("xl", "xh"):
                at = place.get("x")
                index.append(
                    slice(None) if at is None else lax.rem(at, 2) if d == "xl" else lax.div(at, 2)
                )
            else:
                index.append(place.get(d, slice(None)))
        return tuple(index)

    def peer_of(offsets):
        place = {a: lax.rem(coords[a] + j, 4) for a, j in offsets.items()}
        full = dict(coords, **place)
        return device(full["x"], full["y"], full["z"], core), place

    ALL_DIMS = ("xl", "z", "y", "xh")

    def send_line(c, p):
        axis, n = FIRST_AXIS[c][p], c * PARTS + p
        for j in (2, 1, 3):
            peer, place = peer_of({axis: j})
            remote(
                terms_of[n].at[at_peer(ALL_DIMS, place)],
                in_line[n].at[j - 1],
                rs_s.at[2 * n],
                rs_r.at[2 * n],
                peer,
            )
        sent(in_line[n], rs_s.at[2 * n])

    def sum_line(c, p):
        axis, n = FIRST_AXIS[c][p], c * PARTS + p
        own = terms_of[n].at[at_peer(ALL_DIMS, {axis: coords[axis]})]
        arrived(in_line[n], rs_r.at[2 * n])
        total = own[...].astype(F32)
        for j in range(3):
            total = total + in_line[n][j].astype(F32)
        halved[n][...] = total.astype(BF)

    def send_plane(c, p):
        axis, n = FIRST_AXIS[c][p], c * PARTS + p
        u, v = (a for a in ("x", "y", "z") if a != axis)
        for ju in (2, 1, 3, 0):
            for jv in (2, 1, 3, 0):
                if ju or jv:
                    peer, place = peer_of({u: ju, v: jv})
                    remote(
                        halved[n].at[at_peer(left_after(axis), place)],
                        in_plane[n].at[ju * 4 + jv - 1],
                        rs_s.at[2 * n + 1],
                        rs_r.at[2 * n + 1],
                        peer,
                    )
        sent(in_plane[n], rs_s.at[2 * n + 1])

    def sum_plane(c, p):
        axis, n = FIRST_AXIS[c][p], c * PARTS + p
        place = {a: coords[a] for a in ("x", "y", "z") if a != axis}
        arrived(in_plane[n], rs_r.at[2 * n + 1])
        total = halved[n][at_peer(left_after(axis), place)].astype(F32)
        for j in range(15):
            total = total + in_plane[n][j].astype(F32)
        final[c, 16 * p : 16 * (p + 1)] = total.astype(BF)

    def after_line(c):
        for p in range(PARTS):
            sum_line(c, p)
        for p in range(PARTS):
            send_plane(c, p)

    def after_plane(c):
        for p in range(PARTS):
            sum_plane(c, p)
        send_final(c)

    def chunk_terms(c):
        cols = slice(256 * c, 256 * (c + 1))
        Gb[:, cols] = (G[:, cols] * (1.0 / math.sqrt(SDH))).astype(BF)
        for xl_ in range(2):
            terms = (
                jnp.dot(HdT[768 * xl_ : 768 * (xl_ + 1), :], Gb[:, cols], preferred_element_type=F32)
                .astype(BF)
                .reshape(4, 4, PARTS, 16, 256)
            )
            for p in range(PARTS):
                for xh_ in range(2):
                    terms_of[c * PARTS + p][xl_, :, :, xh_] = terms[
                        :, :, p, :, 128 * xh_ : 128 * (xh_ + 1)
                    ]
        for p in range(PARTS):
            send_line(c, p)

    yl = lax.rem(y, 2)
    goal = lax.div(y, 2)

    own_block = core * 4 + yl * 2 + xh

    def send_final(c):
        for j in range(8):
            remote(
                final.at[c],
                agbuf.at[c, own_block],
                ag_s.at[c],
                ag_r.at[c],
                {"dp": lax.rem(dp + j, 8), "ctx": k * 2 + goal},
                None if j else core != goal,
            )
        sent(spare, ag_s.at[c], core == goal)
        sent(agbuf.at[c], ag_s.at[c], core != goal)

        @pl.when(core == goal)
        def _():
            agbuf[c, own_block] = final[c]

    loss = jnp.zeros((1, 128), F32)
    def group_arrives(q):
        h0, h1 = GROUPS_OF_HEADS[q]
        cols = slice(TDH * h0, TDH * h1)
        arrived(Ttail.at[:, cols], tail_r.at[3 + q], has_prev)
        T[tail_rows, cols] = jnp.where(
            tail_mask(TDH * (h1 - h0)), Ttail[:, cols], T[tail_rows, cols]
        )

    starts = [h0 for h0, _ in GROUPS_OF_HEADS]
    group_arrives(0)
    scores(0)
    for h in range(H + 1):
        if h + 1 in starts:
            group_arrives(starts.index(h + 1))
        if h + 1 < H:
            scores(h + 1)
        if h:
            gradient(h - 1)
        if h < H:
            loss = softmaxes(h, loss)
            weigh(h)
        if h - 1 in READY:
            chunk_terms(READY.index(h - 1))

    remote(Gb.at[theirs], GX, tail_s.at[5], tail_r.at[8], pair)
    sent(GX, tail_s.at[5])
    remote(
        Gb.at[tail_rows],
        GT.at[core],
        tail_s.at[6],
        tail_r.at[9 + core],
        {"dp": dp, "ctx": k * 2 - 1},
        has_prev,
    )
    sent(GT.at[0], tail_s.at[6], has_prev)
    lossb[0] = jnp.broadcast_to(loss, (8, 128))
    for j in (1, 2, 3):
        remote(lossb.at[0], lossr.at[j - 1], loss_s.at[0], loss_r.at[0], along("z", j)[0])
    sent(lossr.at[0:3], loss_s.at[0])

    after_line(0)

    w_oth.wait()
    arrived(GX, tail_r.at[8])
    for c in range(2):
        arrived(GT.at[c], tail_r.at[9 + c], sends)
    rows = slice(ROWS - TAIL, ROWS)
    lent = slot((TAIL, SW), SLOTS - TAIL - ROWS + core * ROWS) >= lo
    zero = jnp.zeros((TAIL, SW), BF)
    keep = jnp.full((TAIL, SW), k, jnp.int32) < 7
    own_low = Gb[pl.ds(pl.multiple_of(core * ROWS, ROWS), ROWS - TAIL), :]
    own_high = Gb[pl.ds(pl.multiple_of(core * ROWS + ROWS - TAIL, TAIL), TAIL), :]
    own_high = jnp.where(lent, jnp.where(keep, GT[1], zero), own_high)
    GX[rows, :] = jnp.where(lent, jnp.where(keep, GT[0], zero), GX[rows, :])
    own_rows = jnp.concatenate([own_low, own_high], axis=0)
    for r in range(0, DS, 512):
        out_hidden[:, r : r + 512] = (
            lax.dot_general(own_rows, Wown[r : r + 512, :], nt, preferred_element_type=F32)
            + lax.dot_general(GX[...], Woth[r : r + 512, :], nt, preferred_element_type=F32)
        ).astype(BF)

    after_line(1)
    after_plane(0)

    arrived(lossr.at[0:3], loss_r.at[0])
    lossb[1] = lossb[0] + lossr[0] + lossr[1] + lossr[2]
    x_other = xh * 2 + 1 - xl
    remote(lossb.at[1], lossr.at[3], loss_s.at[1], loss_r.at[1], device(x_other, y, z, core))
    sent(lossr.at[3], loss_s.at[1])

    after_line(2)
    after_plane(1)

    arrived(lossr.at[3], loss_r.at[1])
    lossb[2] = lossb[1] + lossr[3]
    remote(lossb.at[2], lossr.at[4], loss_s.at[2], loss_r.at[2], pair)
    sent(lossr.at[4], loss_s.at[2])

    after_plane(2)

    arrived(lossr.at[4], loss_r.at[2])
    loss_total = lossb[2] + lossr[4]
    out_loss[...] = jnp.broadcast_to(
        jnp.sum(loss_total[:1], axis=1, keepdims=True) * (math.log(2.0) / LOSS_SCALE), (1, 128)
    )

    for c in range(CHUNKS):
        arrived(spare, ag_r.at[c], core == goal)
        arrived(agbuf.at[c], ag_r.at[c], core != goal)
        out_terms[c] = agbuf[c]

    for copy, cond in pending:
        if cond is None:
            copy.wait_send()
        else:
            pl.when(cond)(copy.wait_send)


def finish(loss, hidden_grad, terms, out_loss, out_hidden, out_wq, out_wk):
    out_loss[0] = loss[0, 0]
    out_hidden[...] = hidden_grad[...]
    for r, out in enumerate((out_wq, out_wk)):
        for c in range(CHUNKS):
            for yl in range(2):
                for xh in range(2):
                    at = 256 * c + 128 * xh
                    block = terms[c, r * 4 + yl * 2 + xh]
                    out[48 * yl : 48 * (yl + 1), at : at + 128] = block.astype(F32)


def per_device(teacher_query, teacher_key, student_hidden, weight_query, weight_key, doc_lengths):
    scratch = [
        pltpu.VMEM((SLOTS, TW), BF),
        pltpu.VMEM((TAIL, TW), BF),
        pltpu.VMEM((SLOTS, DS), BF),
        pltpu.VMEM((TAIL, DS), BF),
        pltpu.VMEM((DS, SLOTS), BF),
        pltpu.VMEM((DS, SW), BF),
        pltpu.VMEM((DS, SW), BF),
        pltpu.VMEM((SLOTS, SW), BF),
        pltpu.VMEM((4, SLOTS, SLOTS), F32),
        pltpu.VMEM((2, SLOTS, SLOTS), F32),
        pltpu.VMEM((SLOTS, SW), F32),
        pltpu.VMEM((SLOTS, SW), BF),
        pltpu.VMEM((ROWS, SW), BF),
        pltpu.VMEM((2, TAIL, SW), BF),
        pltpu.VMEM((2, SLOTS, SLOTS), BF),
        pltpu.VMEM((CHUNKS, 8, 48, 128), BF),
        pltpu.VMEM((CHUNKS, 48, 128), BF),
        pltpu.VMEM((3, 8, 128), F32),
        pltpu.VMEM((5, 8, 128), F32),
        pltpu.VMEM((7, 48, 128), BF),
    ]
    firsts = [axis for axes in FIRST_AXIS for axis in axes]
    for _ in firsts:
        scratch.append(pltpu.VMEM(extent(("xl", "z", "y", "xh")) + UNIT, BF))
    for axis in firsts:
        scratch.append(pltpu.VMEM(extent(left_after(axis)) + UNIT, BF))
    for axis in firsts:
        scratch.append(pltpu.VMEM((3,) + extent(left_after(axis)) + UNIT, BF))
    for _ in firsts:
        scratch.append(pltpu.VMEM((15,) + UNIT, BF))
    dma = pltpu.SemaphoreType.DMA
    scratch += [
        dma((4,)),
        dma((7,)),
        dma((12,)),
        dma((18,)),
        dma((18,)),
        dma((3,)),
        dma((3,)),
        dma((3,)),
        dma((3,)),
    ]
    vmem = pl.BlockSpec(memory_space=pltpu.VMEM)
    anywhere = pl.BlockSpec(memory_space=pl.ANY)
    loss, hidden_grad, terms = pl.pallas_call(
        kernel,
        out_shape=(
            jax.ShapeDtypeStruct((1, 128), F32),
            jax.ShapeDtypeStruct((ROWS, DS), BF),
            jax.ShapeDtypeStruct((CHUNKS, 8, 48, 128), BF),
        ),
        in_specs=[anywhere] * 5 + [pl.BlockSpec(memory_space=pltpu.SMEM)],
        out_specs=(vmem, vmem, vmem),
        scratch_shapes=scratch,
        compiler_params=pltpu.CompilerParams(
            collective_id=0, has_side_effects=True, vmem_limit_bytes=56 * 1024 * 1024
        ),
        name="relations",
    )(
        teacher_query[0],
        teacher_key[0],
        student_hidden[0],
        weight_query,
        weight_key,
        doc_lengths,
    )
    smem = pl.BlockSpec(memory_space=pltpu.SMEM)
    loss, hidden_grad, grad_wq, grad_wk = pl.pallas_call(
        finish,
        out_shape=(
            jax.ShapeDtypeStruct((1,), F32),
            jax.ShapeDtypeStruct((ROWS, DS), BF),
            jax.ShapeDtypeStruct((96, SW), F32),
            jax.ShapeDtypeStruct((96, SW), F32),
        ),
        in_specs=[smem, vmem, vmem],
        out_specs=(smem, vmem, vmem, vmem),
        name="finish",
    )(loss, hidden_grad, terms)
    return loss, hidden_grad[None], grad_wq, grad_wk


def solution(mesh):
    in_specs = (
        P("dp", "ctx", None),
        P("dp", "ctx", None),
        P("dp", "ctx", None),
        P(),
        P(),
        P("dp", None),
    )
    out_specs = (P("dp"), P("dp", "ctx", None), P("ctx", None), P("ctx", None))
    return jax.shard_map(
        per_device, mesh=mesh, in_specs=in_specs, out_specs=out_specs, check_vma=False
    )
```

```python
import math

import jax
import jax.numpy as jnp
from jax import lax
from jax.experimental import pallas as pl
from jax.experimental.pallas import tpu as pltpu
from jax.sharding import PartitionSpec as P

H = 16
TDH = 128
SDH = 48
DOCS = 8
ROWS = 128
SLOTS = 256
TAIL = 64
DS = 1536
TW = H * TDH
SW = H * SDH
LOSS_SCALE = 1048576.0
MASKED = -1e30
LOG2E = math.log2(math.e)
BF = jnp.bfloat16
F32 = jnp.float32
MESH = pl.DeviceIdType.MESH

CHUNKS = 3
PARTS = 3
FIRST_AXIS = (("x", "y", "z"), ("x", "y", "z"), ("x", "y", "z"))
READY = (5, 10, 15)
EXTENT = {"xl": 2, "z": 4, "y": 4, "xh": 2}
UNIT = (16, 128)
GROUPS_OF_HEADS = ((0, 4), (4, 8), (8, 12), (12, 14), (14, 16))


def dims_of(axis):
    return ("xl", "xh") if axis == "x" else (axis,)


def left_after(axis):
    return tuple(d for d in ("xl", "z", "y", "xh") if d not in dims_of(axis))


def extent(dims):
    return tuple(EXTENT[d] for d in dims)


def kernel(
    tq,
    tk,
    hid,
    wq,
    wk,
    lengths,
    out_loss,
    out_hidden,
    out_terms,
    T,
    Ttail,
    Hd,
    Htail,
    HdT,
    Wown,
    Woth,
    S,
    X,
    E,
    G,
    Gb,
    GX,
    GT,
    Wb,
    agbuf,
    final,
    lossb,
    lossr,
    spare,
    *rest,
):
    pieces = CHUNKS * PARTS
    terms_of, halved, in_line, in_plane = (
        rest[i * pieces : (i + 1) * pieces] for i in range(4)
    )
    loc, tail_s, tail_r, rs_s, rs_r, ag_s, ag_r, loss_s, loss_r = rest[4 * pieces :]

    dp = lax.axis_index("dp")
    ctx = lax.axis_index("ctx")
    y, xh = lax.div(dp, 2), lax.rem(dp, 2)
    core = lax.rem(ctx, 2)
    k = lax.div(ctx, 2)
    z, xl = lax.rem(k, 4), lax.div(k, 4)
    x = xh * 2 + xl
    coords = {"x": x, "y": y, "z": z}

    def device(x_, y_, z_, core_):
        return {"dp": y_ * 2 + lax.div(x_, 2), "ctx": (lax.rem(x_, 2) * 4 + z_) * 2 + core_}

    def along(axis, j):
        c = dict(coords)
        c[axis] = lax.rem(c[axis] + j, 4)
        return device(c["x"], c["y"], c["z"], core), c[axis]

    pair = {"dp": dp, "ctx": k * 2 + 1 - core}
    is0, is1 = core == 0, core == 1
    has_next, has_prev = k < 7, k > 0
    sends = jnp.logical_and(is1, has_next)

    mine = pl.ds(pl.multiple_of(core * ROWS, ROWS), ROWS)
    theirs = pl.ds(pl.multiple_of((1 - core) * ROWS, ROWS), ROWS)
    own_hidden = pltpu.make_async_copy(hid, Hd.at[mine], loc.at[0])
    own_hidden.start()

    def by_core(first, second, dst, sem):
        def go(src):
            def start():
                pltpu.make_async_copy(src, dst, sem).start()

            return start

        pl.when(is0)(go(first))
        pl.when(is1)(go(second))
        return pltpu.make_async_copy(first, dst, sem)

    w_own = by_core(wq, wk, Wown, loc.at[1])
    own_t = by_core(tq, tk, T.at[mine], loc.at[2])
    w_oth = by_core(wk, wq, Woth, loc.at[3])

    barrier = pltpu.get_barrier_semaphore()

    def hail(device_id):
        pl.semaphore_signal(barrier, inc=1, device_id=device_id, device_id_type=MESH)

    hail(pair)
    for axis in ("x", "y", "z"):
        for j in (1, 2, 3):
            hail(along(axis, j)[0])

    @pl.when(sends)
    def _():
        hail({"dp": dp, "ctx": k * 2 + 2})
        hail({"dp": dp, "ctx": k * 2 + 3})

    @pl.when(has_prev)
    def _():
        hail({"dp": dp, "ctx": k * 2 - 1})

    pl.semaphore_wait(
        barrier, 10 + jnp.where(sends, 2, 0) + jnp.where(has_prev, 1, 0)
    )

    pending = []

    def copy_of(src, dst, send_sem, recv_sem, device_id):
        return pltpu.make_async_remote_copy(
            src_ref=src,
            dst_ref=dst,
            send_sem=send_sem,
            recv_sem=recv_sem,
            device_id=device_id,
            device_id_type=MESH,
        )

    def when(cond, act):
        if cond is None:
            act()
        else:
            pl.when(cond)(act)

    def remote(src, dst, send_sem, recv_sem, device_id, cond=None):
        when(cond, copy_of(src, dst, send_sem, recv_sem, device_id).start)

    def sent(like, send_sem, cond=None):
        pending.append((copy_of(like, like, send_sem, send_sem, pair), cond))

    def arrived(dst, recv_sem, cond=None):
        when(cond, copy_of(dst, dst, recv_sem, recv_sem, pair).wait_recv)

    last = pl.ds(ROWS - TAIL, TAIL)
    half = DS // 2
    remote(hid, Hd.at[mine], tail_s.at[0], tail_r.at[0], pair)
    sent(Hd.at[mine], tail_s.at[0])
    for c in range(2):
        cols = pl.ds(c * half, half)
        remote(
            hid.at[last, cols],
            Htail.at[:, cols],
            tail_s.at[1],
            tail_r.at[1],
            {"dp": dp, "ctx": k * 2 + 2 + c},
            sends,
        )
    sent(Htail, tail_s.at[1], sends)
    remote(tk, T.at[mine], tail_s.at[2], tail_r.at[2], pair, is0)
    remote(tq, T.at[mine], tail_s.at[2], tail_r.at[2], pair, is1)
    sent(T.at[mine], tail_s.at[2])
    for q, (h0, h1) in enumerate(GROUPS_OF_HEADS):
        cols = pl.ds(TDH * h0, TDH * (h1 - h0))
        for c, src in enumerate((tq, tk)):
            remote(
                src.at[last, cols],
                Ttail.at[:, cols],
                tail_s.at[3],
                tail_r.at[3 + q],
                {"dp": dp, "ctx": k * 2 + 2 + c},
                sends,
            )
    sent(T.at[mine], tail_s.at[3], sends)

    start = jnp.int32(0)
    end = jnp.int32(0)
    count = jnp.int32(0)
    for i in range(DOCS):
        value = lengths[0, i]
        start = start + jnp.where(i < k, value, 0)
        end = end + jnp.where(i <= k, value, 0)
        count = count + value
    lo = end - SLOTS * k
    hi = start - SLOTS * (k - 1)
    mean_over = 1.0 / (H * jnp.full((1, 128), count, jnp.int32).astype(F32))
    coefficient = LOSS_SCALE * mean_over

    def slot(shape, first):
        return lax.broadcasted_iota(jnp.int32, shape, 0) + first

    def tail_mask(width):
        return slot((TAIL, width), SLOTS - TAIL) >= hi

    own_hidden.wait()
    w_own.wait()
    arrived(Hd.at[theirs], tail_r.at[0])
    for r in range(0, SLOTS, 128):
        S[r : r + 128, :] = jnp.dot(
            Hd[r : r + 128, :], Wown[...], preferred_element_type=F32
        ).astype(BF)
    my_half = Htail.at[:, pl.ds(pl.multiple_of(core * half, half), half)]
    arrived(my_half, tail_r.at[1], has_prev)
    remote(my_half, my_half, tail_s.at[4], tail_r.at[11], pair, has_prev)
    sent(my_half, tail_s.at[4], has_prev)
    other_half = Htail.at[:, pl.ds(pl.multiple_of((1 - core) * half, half), half)]
    arrived(other_half, tail_r.at[11], has_prev)
    tail_rows = slice(SLOTS - TAIL, SLOTS)
    projected = jnp.dot(Htail[...], Wown[...], preferred_element_type=F32).astype(BF)
    S[tail_rows, :] = jnp.where(tail_mask(SW), projected, S[tail_rows, :])
    Hd[tail_rows, :] = jnp.where(tail_mask(DS), Htail[...], Hd[tail_rows, :])
    for r in range(0, DS, 128):
        HdT[r : r + 128, :] = Hd[:, r : r + 128].T

    own_t.wait()
    arrived(T.at[theirs], tail_r.at[2])

    row_slot = lax.broadcasted_iota(jnp.int32, (SLOTS, 128), 0)
    row_lane = lax.broadcasted_iota(jnp.int32, (SLOTS, 128), 1)
    row_bad = jnp.logical_and(row_slot >= lo, row_slot < hi)
    row_bias = jnp.where(row_bad, MASKED, 0.0)
    bias_tile = jnp.where(row_lane == 0, row_bias, 0.0).astype(BF)
    one_tile = jnp.where(row_lane == 0, 1.0, 0.0).astype(BF)
    bias_all = row_bias.astype(BF)
    rate = []
    for cb in range(2):
        lane_slot = lax.broadcasted_iota(jnp.int32, (1, 128), 1) + 128 * cb
        good = jnp.logical_or(lane_slot < lo, lane_slot >= hi)
        rate.append(jnp.where(good, coefficient, 0.0))
    ct = LOG2E / math.sqrt(TDH)
    cs = LOG2E / math.sqrt(SDH)
    nt = (((1,), (1,)), ((), ()))

    G[...] = jnp.zeros_like(G)

    def probabilities(scores, factor, rate_here):
        high = jnp.max(scores, axis=0, keepdims=True)
        rel = (scores - high) * factor
        raw = jnp.exp2(rel)
        total = jnp.sum(raw, axis=0, keepdims=True)
        return rel, raw * (rate_here / total), jnp.log2(total)

    def student_tiles(h):
        first = SDH * h
        a, b = first // 128, (first + SDH - 1) // 128
        width = (b - a + 1) * 128
        cols = slice(128 * a, 128 * a + width)
        st = S[:, cols]
        lane = lax.broadcasted_iota(jnp.int32, (SLOTS, width), 1) + 128 * a
        inside = jnp.logical_and(lane >= first, lane < first + SDH)
        free = 128 * a if first > 128 * a else 128 * a + width - 1
        return cols, st, jnp.where(inside, st, jnp.zeros_like(st)), lane == free

    def scores(h):
        th = T[:, TDH * h : TDH * (h + 1)]
        X[h % 2] = lax.dot_general(
            jnp.concatenate([th, bias_tile], axis=1),
            jnp.concatenate([th, one_tile], axis=1),
            nt,
            preferred_element_type=F32,
        )
        _, st, picked, free = student_tiles(h)
        bias = jnp.concatenate([bias_all] * (st.shape[1] // 128), axis=1)
        X[2 + h % 2] = lax.dot_general(
            jnp.where(free, bias, picked),
            jnp.where(free, jnp.ones_like(st), st),
            nt,
            preferred_element_type=F32,
        )

    def softmaxes(h, loss):
        for cb in range(2):
            block = slice(128 * cb, 128 * (cb + 1))
            rel_t, et, log_t = probabilities(X[h % 2, :, block], ct, rate[cb])
            rel_s, es, log_s = probabilities(X[2 + h % 2, :, block], cs, rate[cb])
            E[h % 2, :, block] = es - et
            loss = loss + jnp.sum(et * (rel_t - rel_s), axis=0, keepdims=True)
            loss = loss - rate[cb] * (log_t - log_s)
        return loss

    def weigh(h):
        e, w = E.at[h % 2], Wb.at[h % 2]
        cross = e[:128, 128:] + e[128:, :128].T
        for b in range(2):
            block = slice(128 * b, 128 * (b + 1))
            square = e[block, block]
            w[block, block] = (square + square.T).astype(BF)
        w[:128, 128:] = cross.astype(BF)
        w[128:, :128] = cross.T.astype(BF)

    def gradient(h):
        cols, _, picked, _ = student_tiles(h)
        G[:, cols] += jnp.dot(Wb[h % 2], picked, preferred_element_type=F32)

    def at_peer(dims, place):
        index = []
        for d in dims:
            if d in ("xl", "xh"):
                at = place.get("x")
                index.append(
                    slice(None) if at is None else lax.rem(at, 2) if d == "xl" else lax.div(at, 2)
                )
            else:
                index.append(place.get(d, slice(None)))
        return tuple(index)

    def peer_of(offsets):
        place = {a: lax.rem(coords[a] + j, 4) for a, j in offsets.items()}
        full = dict(coords, **place)
        return device(full["x"], full["y"], full["z"], core), place

    ALL_DIMS = ("xl", "z", "y", "xh")

    def send_line(c, p):
        axis, n = FIRST_AXIS[c][p], c * PARTS + p
        for j in (2, 1, 3):
            peer, place = peer_of({axis: j})
            remote(
                terms_of[n].at[at_peer(ALL_DIMS, place)],
                in_line[n].at[j - 1],
                rs_s.at[2 * n],
                rs_r.at[2 * n],
                peer,
            )
        sent(in_line[n], rs_s.at[2 * n])

    def sum_line(c, p):
        axis, n = FIRST_AXIS[c][p], c * PARTS + p
        own = terms_of[n].at[at_peer(ALL_DIMS, {axis: coords[axis]})]
        arrived(in_line[n], rs_r.at[2 * n])
        total = own[...].astype(F32)
        for j in range(3):
            total = total + in_line[n][j].astype(F32)
        halved[n][...] = total.astype(BF)

    def send_plane(c, p):
        axis, n = FIRST_AXIS[c][p], c * PARTS + p
        u, v = (a for a in ("x", "y", "z") if a != axis)
        for ju in (2, 1, 3, 0):
            for jv in (2, 1, 3, 0):
                if ju or jv:
                    peer, place = peer_of({u: ju, v: jv})
                    remote(
                        halved[n].at[at_peer(left_after(axis), place)],
                        in_plane[n].at[ju * 4 + jv - 1],
                        rs_s.at[2 * n + 1],
                        rs_r.at[2 * n + 1],
                        peer,
                    )
        sent(in_plane[n], rs_s.at[2 * n + 1])

    def sum_plane(c, p):
        axis, n = FIRST_AXIS[c][p], c * PARTS + p
        place = {a: coords[a] for a in ("x", "y", "z") if a != axis}
        arrived(in_plane[n], rs_r.at[2 * n + 1])
        total = halved[n][at_peer(left_after(axis), place)].astype(F32)
        for j in range(15):
            total = total + in_plane[n][j].astype(F32)
        final[c, 16 * p : 16 * (p + 1)] = total.astype(BF)

    def after_line(c):
        for p in range(PARTS):
            sum_line(c, p)
        for p in range(PARTS):
            send_plane(c, p)

    def after_plane(c):
        for p in range(PARTS):
            sum_plane(c, p)
        send_final(c)

    def chunk_terms(c):
        cols = slice(256 * c, 256 * (c + 1))
        Gb[:, cols] = (G[:, cols] * (1.0 / math.sqrt(SDH))).astype(BF)
        for xl_ in range(2):
            terms = (
                jnp.dot(HdT[768 * xl_ : 768 * (xl_ + 1), :], Gb[:, cols], preferred_element_type=F32)
                .astype(BF)
                .reshape(4, 4, PARTS, 16, 256)
            )
            for p in range(PARTS):
                for xh_ in range(2):
                    terms_of[c * PARTS + p][xl_, :, :, xh_] = terms[
                        :, :, p, :, 128 * xh_ : 128 * (xh_ + 1)
                    ]
        for p in range(PARTS):
            send_line(c, p)

    yl = lax.rem(y, 2)
    goal = lax.div(y, 2)

    own_block = core * 4 + yl * 2 + xh

    def send_final(c):
        for j in range(8):
            remote(
                final.at[c],
                agbuf.at[c, own_block],
                ag_s.at[c],
                ag_r.at[c],
                {"dp": lax.rem(dp + j, 8), "ctx": k * 2 + goal},
                None if j else core != goal,
            )
        sent(spare, ag_s.at[c], core == goal)
        sent(agbuf.at[c], ag_s.at[c], core != goal)

        @pl.when(core == goal)
        def _():
            agbuf[c, own_block] = final[c]

    loss = jnp.zeros((1, 128), F32)
    def group_arrives(q):
        h0, h1 = GROUPS_OF_HEADS[q]
        cols = slice(TDH * h0, TDH * h1)
        arrived(Ttail.at[:, cols], tail_r.at[3 + q], has_prev)
        T[tail_rows, cols] = jnp.where(
            tail_mask(TDH * (h1 - h0)), Ttail[:, cols], T[tail_rows, cols]
        )

    starts = [h0 for h0, _ in GROUPS_OF_HEADS]
    group_arrives(0)
    scores(0)
    for h in range(H + 1):
        if h + 1 in starts:
            group_arrives(starts.index(h + 1))
        if h + 1 < H:
            scores(h + 1)
        if h:
            gradient(h - 1)
        if h < H:
            loss = softmaxes(h, loss)
            weigh(h)
        if h - 1 in READY:
            chunk_terms(READY.index(h - 1))

    lossb[0] = jnp.broadcast_to(loss, (8, 128))
    for j in (1, 2, 3):
        remote(lossb.at[0], lossr.at[j - 1], loss_s.at[0], loss_r.at[0], along("z", j)[0])
    sent(lossr.at[0:3], loss_s.at[0])

    after_line(0)

    after_line(1)
    after_line(2)
    remote(Gb.at[theirs], GX, tail_s.at[5], tail_r.at[8], pair)
    sent(GX, tail_s.at[5])
    remote(
        Gb.at[tail_rows],
        GT.at[core],
        tail_s.at[6],
        tail_r.at[9 + core],
        {"dp": dp, "ctx": k * 2 - 1},
        has_prev,
    )
    sent(GT.at[0], tail_s.at[6], has_prev)

    arrived(lossr.at[0:3], loss_r.at[0])
    lossb[1] = lossb[0] + lossr[0] + lossr[1] + lossr[2]
    x_other = xh * 2 + 1 - xl
    remote(lossb.at[1], lossr.at[3], loss_s.at[1], loss_r.at[1], device(x_other, y, z, core))
    sent(lossr.at[3], loss_s.at[1])

    after_plane(0)
    after_plane(1)

    arrived(lossr.at[3], loss_r.at[1])
    lossb[2] = lossb[1] + lossr[3]
    remote(lossb.at[2], lossr.at[4], loss_s.at[2], loss_r.at[2], pair)
    sent(lossr.at[4], loss_s.at[2])

    after_plane(2)

    w_oth.wait()
    arrived(GX, tail_r.at[8])
    for c in range(2):
        arrived(GT.at[c], tail_r.at[9 + c], sends)
    rows = slice(ROWS - TAIL, ROWS)
    lent = slot((TAIL, SW), SLOTS - TAIL - ROWS + core * ROWS) >= lo
    zero = jnp.zeros((TAIL, SW), BF)
    keep = jnp.full((TAIL, SW), k, jnp.int32) < 7
    own_low = Gb[pl.ds(pl.multiple_of(core * ROWS, ROWS), ROWS - TAIL), :]
    own_high = Gb[pl.ds(pl.multiple_of(core * ROWS + ROWS - TAIL, TAIL), TAIL), :]
    own_high = jnp.where(lent, jnp.where(keep, GT[1], zero), own_high)
    GX[rows, :] = jnp.where(lent, jnp.where(keep, GT[0], zero), GX[rows, :])
    own_rows = jnp.concatenate([own_low, own_high], axis=0)
    for r in range(0, DS, 512):
        out_hidden[:, r : r + 512] = (
            lax.dot_general(own_rows, Wown[r : r + 512, :], nt, preferred_element_type=F32)
            + lax.dot_general(GX[...], Woth[r : r + 512, :], nt, preferred_element_type=F32)
        ).astype(BF)

    arrived(lossr.at[4], loss_r.at[2])
    loss_total = lossb[2] + lossr[4]
    out_loss[...] = jnp.broadcast_to(
        jnp.sum(loss_total[:1], axis=1, keepdims=True) * (math.log(2.0) / LOSS_SCALE), (1, 128)
    )

    for c in range(CHUNKS):
        arrived(spare, ag_r.at[c], core == goal)
        arrived(agbuf.at[c], ag_r.at[c], core != goal)
        out_terms[c] = agbuf[c]

    for copy, cond in pending:
        if cond is None:
            copy.wait_send()
        else:
            pl.when(cond)(copy.wait_send)


def finish(loss, hidden_grad, terms, out_loss, out_hidden, out_wq, out_wk):
    out_loss[0] = loss[0, 0]
    out_hidden[...] = hidden_grad[...]
    for r, out in enumerate((out_wq, out_wk)):
        for c in range(CHUNKS):
            for yl in range(2):
                for xh in range(2):
                    at = 256 * c + 128 * xh
                    block = terms[c, r * 4 + yl * 2 + xh]
                    out[48 * yl : 48 * (yl + 1), at : at + 128] = block.astype(F32)


def per_device(teacher_query, teacher_key, student_hidden, weight_query, weight_key, doc_lengths):
    scratch = [
        pltpu.VMEM((SLOTS, TW), BF),
        pltpu.VMEM((TAIL, TW), BF),
        pltpu.VMEM((SLOTS, DS), BF),
        pltpu.VMEM((TAIL, DS), BF),
        pltpu.VMEM((DS, SLOTS), BF),
        pltpu.VMEM((DS, SW), BF),
        pltpu.VMEM((DS, SW), BF),
        pltpu.VMEM((SLOTS, SW), BF),
        pltpu.VMEM((4, SLOTS, SLOTS), F32),
        pltpu.VMEM((2, SLOTS, SLOTS), F32),
        pltpu.VMEM((SLOTS, SW), F32),
        pltpu.VMEM((SLOTS, SW), BF),
        pltpu.VMEM((ROWS, SW), BF),
        pltpu.VMEM((2, TAIL, SW), BF),
        pltpu.VMEM((2, SLOTS, SLOTS), BF),
        pltpu.VMEM((CHUNKS, 8, 48, 128), BF),
        pltpu.VMEM((CHUNKS, 48, 128), BF),
        pltpu.VMEM((3, 8, 128), F32),
        pltpu.VMEM((5, 8, 128), F32),
        pltpu.VMEM((7, 48, 128), BF),
    ]
    firsts = [axis for axes in FIRST_AXIS for axis in axes]
    for _ in firsts:
        scratch.append(pltpu.VMEM(extent(("xl", "z", "y", "xh")) + UNIT, BF))
    for axis in firsts:
        scratch.append(pltpu.VMEM(extent(left_after(axis)) + UNIT, BF))
    for axis in firsts:
        scratch.append(pltpu.VMEM((3,) + extent(left_after(axis)) + UNIT, BF))
    for _ in firsts:
        scratch.append(pltpu.VMEM((15,) + UNIT, BF))
    dma = pltpu.SemaphoreType.DMA
    scratch += [
        dma((4,)),
        dma((7,)),
        dma((12,)),
        dma((18,)),
        dma((18,)),
        dma((3,)),
        dma((3,)),
        dma((3,)),
        dma((3,)),
    ]
    vmem = pl.BlockSpec(memory_space=pltpu.VMEM)
    anywhere = pl.BlockSpec(memory_space=pl.ANY)
    loss, hidden_grad, terms = pl.pallas_call(
        kernel,
        out_shape=(
            jax.ShapeDtypeStruct((1, 128), F32),
            jax.ShapeDtypeStruct((ROWS, DS), BF),
            jax.ShapeDtypeStruct((CHUNKS, 8, 48, 128), BF),
        ),
        in_specs=[anywhere] * 5 + [pl.BlockSpec(memory_space=pltpu.SMEM)],
        out_specs=(vmem, vmem, vmem),
        scratch_shapes=scratch,
        compiler_params=pltpu.CompilerParams(
            collective_id=0, has_side_effects=True, vmem_limit_bytes=56 * 1024 * 1024
        ),
        name="relations",
    )(
        teacher_query[0],
        teacher_key[0],
        student_hidden[0],
        weight_query,
        weight_key,
        doc_lengths,
    )
    smem = pl.BlockSpec(memory_space=pltpu.SMEM)
    loss, hidden_grad, grad_wq, grad_wk = pl.pallas_call(
        finish,
        out_shape=(
            jax.ShapeDtypeStruct((1,), F32),
            jax.ShapeDtypeStruct((ROWS, DS), BF),
            jax.ShapeDtypeStruct((96, SW), F32),
            jax.ShapeDtypeStruct((96, SW), F32),
        ),
        in_specs=[smem, vmem, vmem],
        out_specs=(smem, vmem, vmem, vmem),
        name="finish",
    )(loss, hidden_grad, terms)
    return loss, hidden_grad[None], grad_wq, grad_wk


def solution(mesh):
    in_specs = (
        P("dp", "ctx", None),
        P("dp", "ctx", None),
        P("dp", "ctx", None),
        P(),
        P(),
        P("dp", None),
    )
    out_specs = (P("dp"), P("dp", "ctx", None), P("ctx", None), P("ctx", None))
    return jax.shard_map(
        per_device, mesh=mesh, in_specs=in_specs, out_specs=out_specs, check_vma=False
    )
```

```python
import math

import jax
import jax.numpy as jnp
from jax import lax
from jax.experimental import pallas as pl
from jax.experimental.pallas import tpu as pltpu
from jax.sharding import PartitionSpec as P

H = 16
TDH = 128
SDH = 48
DOCS = 8
ROWS = 128
SLOTS = 256
TAIL = 64
DS = 1536
TW = H * TDH
SW = H * SDH
LOSS_SCALE = 1048576.0
MASKED = -1e30
LOG2E = math.log2(math.e)
BF = jnp.bfloat16
F32 = jnp.float32
MESH = pl.DeviceIdType.MESH

CHUNKS = 3
PARTS = 3
FIRST_AXIS = ("x", "y", "z")
TILE_OF_HEAD = {(128 * (t + 1) - 1) // SDH: t for t in range(2 * CHUNKS)}
EXTENT = {"xl": 2, "z": 4, "y": 4, "xh": 2}
UNIT = (16, 128)
GROUPS_OF_HEADS = ((0, 4), (4, 8), (8, 12), (12, 14), (14, 16))


def dims_of(axis):
    return ("xl", "xh") if axis == "x" else (axis,)


def left_after(axis):
    return tuple(d for d in ("xl", "z", "y", "xh") if d not in dims_of(axis))


def extent(dims):
    return tuple(EXTENT[d] for d in dims)


def kernel(
    tq,
    tk,
    hid,
    wq,
    wk,
    lengths_in,
    out_loss,
    out_hidden,
    out_terms,
    lengths,
    T,
    Ttail,
    Hd,
    Htail,
    HdT,
    Wown,
    Woth,
    S,
    X,
    E,
    G,
    Gb,
    GX,
    GT,
    Wb,
    agbuf,
    final,
    lossb,
    lossr,
    spare,
    *rest,
):
    pieces = CHUNKS * PARTS
    terms_of, halved, in_line, in_plane = (
        rest[i * pieces : (i + 1) * pieces] for i in range(4)
    )
    loc, tail_s, tail_r, rs_s, rs_r, ag_s, ag_r, loss_s, loss_r = rest[4 * pieces :]

    dp = lax.axis_index("dp")
    ctx = lax.axis_index("ctx")
    y, xh = lax.div(dp, 2), lax.rem(dp, 2)
    core = lax.rem(ctx, 2)
    k = lax.div(ctx, 2)
    z, xl = lax.rem(k, 4), lax.div(k, 4)
    x = xh * 2 + xl
    coords = {"x": x, "y": y, "z": z}

    def device(x_, y_, z_, core_):
        return {"dp": y_ * 2 + lax.div(x_, 2), "ctx": (lax.rem(x_, 2) * 4 + z_) * 2 + core_}

    def along(axis, j):
        c = dict(coords)
        c[axis] = lax.rem(c[axis] + j, 4)
        return device(c["x"], c["y"], c["z"], core), c[axis]

    pair = {"dp": dp, "ctx": k * 2 + 1 - core}
    is0, is1 = core == 0, core == 1
    has_next, has_prev = k < 7, k > 0
    sends = jnp.logical_and(is1, has_next)

    mine = pl.ds(pl.multiple_of(core * ROWS, ROWS), ROWS)
    theirs = pl.ds(pl.multiple_of((1 - core) * ROWS, ROWS), ROWS)
    own_hidden = pltpu.make_async_copy(hid, Hd.at[mine], loc.at[0])
    own_hidden.start()
    get_lengths = pltpu.make_async_copy(lengths_in, lengths, loc.at[4])
    get_lengths.start()

    def by_core(first, second, dst, sem):
        def go(src):
            def start():
                pltpu.make_async_copy(src, dst, sem).start()

            return start

        pl.when(is0)(go(first))
        pl.when(is1)(go(second))
        return pltpu.make_async_copy(first, dst, sem)

    w_own = by_core(wq, wk, Wown, loc.at[1])
    own_t = by_core(tq, tk, T.at[mine], loc.at[2])
    w_oth = by_core(wk, wq, Woth, loc.at[3])

    barrier = pltpu.get_barrier_semaphore()

    def hail(device_id):
        pl.semaphore_signal(barrier, inc=1, device_id=device_id, device_id_type=MESH)

    hail(pair)
    for axis in ("x", "y", "z"):
        for j in (1, 2, 3):
            hail(along(axis, j)[0])

    @pl.when(sends)
    def _():
        hail({"dp": dp, "ctx": k * 2 + 2})
        hail({"dp": dp, "ctx": k * 2 + 3})

    @pl.when(has_prev)
    def _():
        hail({"dp": dp, "ctx": k * 2 - 1})

    pl.semaphore_wait(
        barrier, 10 + jnp.where(sends, 2, 0) + jnp.where(has_prev, 1, 0)
    )

    pending = []

    def copy_of(src, dst, send_sem, recv_sem, device_id):
        return pltpu.make_async_remote_copy(
            src_ref=src,
            dst_ref=dst,
            send_sem=send_sem,
            recv_sem=recv_sem,
            device_id=device_id,
            device_id_type=MESH,
        )

    def when(cond, act):
        if cond is None:
            act()
        else:
            pl.when(cond)(act)

    def remote(src, dst, send_sem, recv_sem, device_id, cond=None):
        when(cond, copy_of(src, dst, send_sem, recv_sem, device_id).start)

    def sent(like, send_sem, cond=None):
        pending.append((copy_of(like, like, send_sem, send_sem, pair), cond))

    def arrived(dst, recv_sem, cond=None):
        when(cond, copy_of(dst, dst, recv_sem, recv_sem, pair).wait_recv)

    last = pl.ds(ROWS - TAIL, TAIL)
    half = DS // 2
    for c in range(2):
        cols = pl.ds(c * half, half)
        remote(
            hid.at[last, cols],
            Htail.at[:, cols],
            tail_s.at[1],
            tail_r.at[1],
            {"dp": dp, "ctx": k * 2 + 2 + c},
            sends,
        )
    sent(Htail, tail_s.at[1], sends)
    remote(hid, Hd.at[mine], tail_s.at[0], tail_r.at[0], pair)
    sent(Hd.at[mine], tail_s.at[0])
    for q, (h0, h1) in enumerate(GROUPS_OF_HEADS):
        cols = pl.ds(TDH * h0, TDH * (h1 - h0))
        for c, src in enumerate((tq, tk)):
            remote(
                src.at[last, cols],
                Ttail.at[:, cols],
                tail_s.at[3],
                tail_r.at[3 + q],
                {"dp": dp, "ctx": k * 2 + 2 + c},
                sends,
            )
    sent(T.at[mine], tail_s.at[3], sends)
    remote(tk, T.at[mine], tail_s.at[2], tail_r.at[2], pair, is0)
    remote(tq, T.at[mine], tail_s.at[2], tail_r.at[2], pair, is1)
    sent(T.at[mine], tail_s.at[2])

    get_lengths.wait()
    start = jnp.int32(0)
    end = jnp.int32(0)
    count = jnp.int32(0)
    for i in range(DOCS):
        value = lengths[0, i]
        start = start + jnp.where(i < k, value, 0)
        end = end + jnp.where(i <= k, value, 0)
        count = count + value
    lo = end - SLOTS * k
    hi = start - SLOTS * (k - 1)
    mean_over = 1.0 / (H * jnp.full((1, 128), count, jnp.int32).astype(F32))
    coefficient = LOSS_SCALE * mean_over

    def slot(shape, first):
        return lax.broadcasted_iota(jnp.int32, shape, 0) + first

    def tail_mask(width):
        return slot((TAIL, width), SLOTS - TAIL) >= hi

    own_hidden.wait()
    w_own.wait()
    arrived(Hd.at[theirs], tail_r.at[0])
    for r in range(0, SLOTS, 128):
        S[r : r + 128, :] = jnp.dot(
            Hd[r : r + 128, :], Wown[...], preferred_element_type=F32
        ).astype(BF)
    my_half = Htail.at[:, pl.ds(pl.multiple_of(core * half, half), half)]
    arrived(my_half, tail_r.at[1], has_prev)
    remote(my_half, my_half, tail_s.at[4], tail_r.at[11], pair, has_prev)
    sent(my_half, tail_s.at[4], has_prev)
    other_half = Htail.at[:, pl.ds(pl.multiple_of((1 - core) * half, half), half)]
    arrived(other_half, tail_r.at[11], has_prev)
    tail_rows = slice(SLOTS - TAIL, SLOTS)
    projected = jnp.dot(Htail[...], Wown[...], preferred_element_type=F32).astype(BF)
    S[tail_rows, :] = jnp.where(tail_mask(SW), projected, S[tail_rows, :])
    Hd[tail_rows, :] = jnp.where(tail_mask(DS), Htail[...], Hd[tail_rows, :])
    for r in range(0, DS, 128):
        HdT[r : r + 128, :] = Hd[:, r : r + 128].T

    own_t.wait()
    arrived(T.at[theirs], tail_r.at[2])

    row_slot = lax.broadcasted_iota(jnp.int32, (SLOTS, 128), 0)
    row_lane = lax.broadcasted_iota(jnp.int32, (SLOTS, 128), 1)
    row_bad = jnp.logical_and(row_slot >= lo, row_slot < hi)
    row_bias = jnp.where(row_bad, MASKED, 0.0)
    bias_tile = jnp.where(row_lane == 0, row_bias, 0.0).astype(BF)
    one_tile = jnp.where(row_lane == 0, 1.0, 0.0).astype(BF)
    bias_all = row_bias.astype(BF)
    rate = []
    for cb in range(2):
        lane_slot = lax.broadcasted_iota(jnp.int32, (1, 128), 1) + 128 * cb
        good = jnp.logical_or(lane_slot < lo, lane_slot >= hi)
        rate.append(jnp.where(good, coefficient, 0.0))
    ct = LOG2E / math.sqrt(TDH)
    cs = LOG2E / math.sqrt(SDH)
    nt = (((1,), (1,)), ((), ()))

    G[...] = jnp.zeros_like(G)

    def probabilities(scores, factor, rate_here):
        high = jnp.max(scores, axis=0, keepdims=True)
        rel = (scores - high) * factor
        raw = jnp.exp2(rel)
        total = jnp.sum(raw, axis=0, keepdims=True)
        return rel, raw * (rate_here / total), jnp.log2(total)

    def student_tiles(h):
        first = SDH * h
        a, b = first // 128, (first + SDH - 1) // 128
        width = (b - a + 1) * 128
        cols = slice(128 * a, 128 * a + width)
        st = S[:, cols]
        lane = lax.broadcasted_iota(jnp.int32, (SLOTS, width), 1) + 128 * a
        inside = jnp.logical_and(lane >= first, lane < first + SDH)
        free = 128 * a if first > 128 * a else 128 * a + width - 1
        return cols, st, jnp.where(inside, st, jnp.zeros_like(st)), lane == free

    def scores(h):
        th = T[:, TDH * h : TDH * (h + 1)]
        X[h % 2] = lax.dot_general(
            jnp.concatenate([th, bias_tile], axis=1),
            jnp.concatenate([th, one_tile], axis=1),
            nt,
            preferred_element_type=F32,
        )
        _, st, picked, free = student_tiles(h)
        bias = jnp.concatenate([bias_all] * (st.shape[1] // 128), axis=1)
        X[2 + h % 2] = lax.dot_general(
            jnp.where(free, bias, picked),
            jnp.where(free, jnp.ones_like(st), st),
            nt,
            preferred_element_type=F32,
        )

    def softmaxes(h, loss):
        for cb in range(2):
            block = slice(128 * cb, 128 * (cb + 1))
            rel_t, et, log_t = probabilities(X[h % 2, :, block], ct, rate[cb])
            rel_s, es, log_s = probabilities(X[2 + h % 2, :, block], cs, rate[cb])
            E[h % 2, :, block] = es - et
            loss = loss + jnp.sum(et * (rel_t - rel_s), axis=0, keepdims=True)
            loss = loss - rate[cb] * (log_t - log_s)
        return loss

    def weigh(h):
        e, w = E.at[h % 2], Wb.at[h % 2]
        cross = e[:128, 128:] + e[128:, :128].T
        for b in range(2):
            block = slice(128 * b, 128 * (b + 1))
            square = e[block, block]
            w[block, block] = (square + square.T).astype(BF)
        w[:128, 128:] = cross.astype(BF)
        w[128:, :128] = cross.T.astype(BF)

    def gradient(h):
        cols, _, picked, _ = student_tiles(h)
        G[:, cols] += jnp.dot(Wb[h % 2], picked, preferred_element_type=F32)

    def at_peer(dims, place):
        index = []
        for d in dims:
            if d in ("xl", "xh"):
                at = place.get("x")
                index.append(
                    slice(None) if at is None else lax.rem(at, 2) if d == "xl" else lax.div(at, 2)
                )
            else:
                index.append(place.get(d, slice(None)))
        return tuple(index)

    def peer_of(offsets):
        place = {a: lax.rem(coords[a] + j, 4) for a, j in offsets.items()}
        full = dict(coords, **place)
        return device(full["x"], full["y"], full["z"], core), place

    ALL_DIMS = ("xl", "z", "y", "xh")

    def send_line(c, p, half_):
        axis, n = FIRST_AXIS[p], c * PARTS + p
        for j in (2, 1, 3):
            peer, place = peer_of({axis: j})
            index = at_peer(ALL_DIMS, place)
            dst = in_line[n].at[j - 1]
            if axis == "x":
                cond = lax.div(place["x"], 2) == half_
            else:
                cond = None
                index = index[:3] + (half_,)
                dst = dst.at[:, :, half_]
            remote(terms_of[n].at[index], dst, rs_s.at[2 * n], rs_r.at[2 * n], peer, cond)

    def sum_line(c, p):
        axis, n = FIRST_AXIS[p], c * PARTS + p
        sent(in_line[n], rs_s.at[2 * n])
        own = terms_of[n].at[at_peer(ALL_DIMS, {axis: coords[axis]})]
        arrived(in_line[n], rs_r.at[2 * n])
        total = own[...].astype(F32)
        for j in range(3):
            total = total + in_line[n][j].astype(F32)
        halved[n][...] = total.astype(BF)

    def send_plane(c, p):
        axis, n = FIRST_AXIS[p], c * PARTS + p
        u, v = (a for a in ("x", "y", "z") if a != axis)
        for ju in (2, 1, 3, 0):
            for jv in (2, 1, 3, 0):
                if ju or jv:
                    peer, place = peer_of({u: ju, v: jv})
                    remote(
                        halved[n].at[at_peer(left_after(axis), place)],
                        in_plane[n].at[ju * 4 + jv - 1],
                        rs_s.at[2 * n + 1],
                        rs_r.at[2 * n + 1],
                        peer,
                    )
        sent(in_plane[n], rs_s.at[2 * n + 1])

    def sum_plane(c, p):
        axis, n = FIRST_AXIS[p], c * PARTS + p
        place = {a: coords[a] for a in ("x", "y", "z") if a != axis}
        arrived(in_plane[n], rs_r.at[2 * n + 1])
        total = halved[n][at_peer(left_after(axis), place)].astype(F32)
        for j in range(15):
            total = total + in_plane[n][j].astype(F32)
        final[c, 16 * p : 16 * (p + 1)] = total.astype(BF)

    def after_line(c):
        for p in range(PARTS):
            sum_line(c, p)
            if c:
                send_plane(c, p)
        if c == 0:
            for p in range(PARTS):
                send_plane(c, p)

    def after_plane(c):
        for p in range(PARTS):
            sum_plane(c, p)
        send_final(c)

    def tile_terms(t):
        c, half_ = t // 2, t % 2
        cols = slice(128 * t, 128 * (t + 1))
        Gb[:, cols] = (G[:, cols] * (1.0 / math.sqrt(SDH))).astype(BF)
        for xl_ in range(2):
            terms = (
                jnp.dot(HdT[768 * xl_ : 768 * (xl_ + 1), :], Gb[:, cols], preferred_element_type=F32)
                .astype(BF)
                .reshape(4, 4, PARTS, 16, 128)
            )
            for p in range(PARTS):
                terms_of[c * PARTS + p][xl_, :, :, half_] = terms[:, :, p]
        for p in range(PARTS):
            send_line(c, p, half_)

    yl = lax.rem(y, 2)
    goal = lax.div(y, 2)

    own_block = core * 4 + yl * 2 + xh

    def send_final(c):
        for j in range(8):
            remote(
                final.at[c],
                agbuf.at[c, own_block],
                ag_s.at[c],
                ag_r.at[c],
                {"dp": lax.rem(dp + j, 8), "ctx": k * 2 + goal},
                None if j else core != goal,
            )
        sent(spare, ag_s.at[c], core == goal)
        sent(agbuf.at[c], ag_s.at[c], core != goal)

        @pl.when(core == goal)
        def _():
            agbuf[c, own_block] = final[c]

    loss = jnp.zeros((1, 128), F32)
    def group_arrives(q):
        h0, h1 = GROUPS_OF_HEADS[q]
        cols = slice(TDH * h0, TDH * h1)
        arrived(Ttail.at[:, cols], tail_r.at[3 + q], has_prev)
        T[tail_rows, cols] = jnp.where(
            tail_mask(TDH * (h1 - h0)), Ttail[:, cols], T[tail_rows, cols]
        )

    starts = [h0 for h0, _ in GROUPS_OF_HEADS]
    group_arrives(0)
    scores(0)
    for h in range(H + 1):
        if h + 1 in starts:
            group_arrives(starts.index(h + 1))
        if h + 1 < H:
            scores(h + 1)
        if h:
            gradient(h - 1)
        if h < H:
            loss = softmaxes(h, loss)
            weigh(h)
        if h - 1 in TILE_OF_HEAD:
            tile_terms(TILE_OF_HEAD[h - 1])

    lossb[0] = jnp.broadcast_to(loss, (8, 128))
    for j in (1, 2, 3):
        remote(lossb.at[0], lossr.at[j - 1], loss_s.at[0], loss_r.at[0], along("z", j)[0])
    sent(lossr.at[0:3], loss_s.at[0])

    after_line(0)

    remote(Gb.at[theirs], GX, tail_s.at[5], tail_r.at[8], pair)
    sent(GX, tail_s.at[5])
    remote(
        Gb.at[tail_rows],
        GT.at[core],
        tail_s.at[6],
        tail_r.at[9 + core],
        {"dp": dp, "ctx": k * 2 - 1},
        has_prev,
    )
    sent(GT.at[0], tail_s.at[6], has_prev)

    after_line(1)
    after_line(2)
    arrived(lossr.at[0:3], loss_r.at[0])
    lossb[1] = lossb[0] + lossr[0] + lossr[1] + lossr[2]
    x_other = xh * 2 + 1 - xl
    remote(lossb.at[1], lossr.at[3], loss_s.at[1], loss_r.at[1], device(x_other, y, z, core))
    sent(lossr.at[3], loss_s.at[1])

    w_oth.wait()
    arrived(GX, tail_r.at[8])
    for c in range(2):
        arrived(GT.at[c], tail_r.at[9 + c], sends)
    rows = slice(ROWS - TAIL, ROWS)
    lent = slot((TAIL, SW), SLOTS - TAIL - ROWS + core * ROWS) >= lo
    zero = jnp.zeros((TAIL, SW), BF)
    keep = jnp.full((TAIL, SW), k, jnp.int32) < 7
    own_low = Gb[pl.ds(pl.multiple_of(core * ROWS, ROWS), ROWS - TAIL), :]
    own_high = Gb[pl.ds(pl.multiple_of(core * ROWS + ROWS - TAIL, TAIL), TAIL), :]
    own_high = jnp.where(lent, jnp.where(keep, GT[1], zero), own_high)
    GX[rows, :] = jnp.where(lent, jnp.where(keep, GT[0], zero), GX[rows, :])
    own_rows = jnp.concatenate([own_low, own_high], axis=0)
    for r in range(0, DS, 512):
        out_hidden[:, r : r + 512] = (
            lax.dot_general(own_rows, Wown[r : r + 512, :], nt, preferred_element_type=F32)
            + lax.dot_general(GX[...], Woth[r : r + 512, :], nt, preferred_element_type=F32)
        ).astype(BF)

    after_plane(0)
    after_plane(1)

    arrived(lossr.at[3], loss_r.at[1])
    lossb[2] = lossb[1] + lossr[3]
    remote(lossb.at[2], lossr.at[4], loss_s.at[2], loss_r.at[2], pair)
    sent(lossr.at[4], loss_s.at[2])

    after_plane(2)

    arrived(lossr.at[4], loss_r.at[2])
    loss_total = lossb[2] + lossr[4]
    out_loss[...] = jnp.broadcast_to(
        jnp.sum(loss_total[:1], axis=1, keepdims=True) * (math.log(2.0) / LOSS_SCALE), (1, 128)
    )

    for c in range(CHUNKS):
        arrived(spare, ag_r.at[c], core == goal)
        arrived(agbuf.at[c], ag_r.at[c], core != goal)
        out_terms[c] = agbuf[c]

    for copy, cond in pending:
        if cond is None:
            copy.wait_send()
        else:
            pl.when(cond)(copy.wait_send)


def finish(loss, hidden_grad, terms, out_loss, out_hidden, out_wq, out_wk):
    out_loss[0] = loss[0, 0]
    out_hidden[...] = hidden_grad[...]
    for r, out in enumerate((out_wq, out_wk)):
        for c in range(CHUNKS):
            for yl in range(2):
                for xh in range(2):
                    at = 256 * c + 128 * xh
                    block = terms[c, r * 4 + yl * 2 + xh]
                    out[48 * yl : 48 * (yl + 1), at : at + 128] = block.astype(F32)


def per_device(teacher_query, teacher_key, student_hidden, weight_query, weight_key, doc_lengths):
    scratch = [
        pltpu.SMEM((1, DOCS), jnp.int32),
        pltpu.VMEM((SLOTS, TW), BF),
        pltpu.VMEM((TAIL, TW), BF),
        pltpu.VMEM((SLOTS, DS), BF),
        pltpu.VMEM((TAIL, DS), BF),
        pltpu.VMEM((DS, SLOTS), BF),
        pltpu.VMEM((DS, SW), BF),
        pltpu.VMEM((DS, SW), BF),
        pltpu.VMEM((SLOTS, SW), BF),
        pltpu.VMEM((4, SLOTS, SLOTS), F32),
        pltpu.VMEM((2, SLOTS, SLOTS), F32),
        pltpu.VMEM((SLOTS, SW), F32),
        pltpu.VMEM((SLOTS, SW), BF),
        pltpu.VMEM((ROWS, SW), BF),
        pltpu.VMEM((2, TAIL, SW), BF),
        pltpu.VMEM((2, SLOTS, SLOTS), BF),
        pltpu.VMEM((CHUNKS, 8, 48, 128), BF),
        pltpu.VMEM((CHUNKS, 48, 128), BF),
        pltpu.VMEM((3, 8, 128), F32),
        pltpu.VMEM((5, 8, 128), F32),
        pltpu.VMEM((7, 48, 128), BF),
    ]
    firsts = FIRST_AXIS * CHUNKS
    for _ in firsts:
        scratch.append(pltpu.VMEM(extent(("xl", "z", "y", "xh")) + UNIT, BF))
    for axis in firsts:
        scratch.append(pltpu.VMEM(extent(left_after(axis)) + UNIT, BF))
    for axis in firsts:
        scratch.append(pltpu.VMEM((3,) + extent(left_after(axis)) + UNIT, BF))
    for _ in firsts:
        scratch.append(pltpu.VMEM((15,) + UNIT, BF))
    dma = pltpu.SemaphoreType.DMA
    scratch += [
        dma((5,)),
        dma((7,)),
        dma((12,)),
        dma((18,)),
        dma((18,)),
        dma((3,)),
        dma((3,)),
        dma((3,)),
        dma((3,)),
    ]
    vmem = pl.BlockSpec(memory_space=pltpu.VMEM)
    anywhere = pl.BlockSpec(memory_space=pl.ANY)
    loss, hidden_grad, terms = pl.pallas_call(
        kernel,
        out_shape=(
            jax.ShapeDtypeStruct((1, 128), F32),
            jax.ShapeDtypeStruct((ROWS, DS), BF),
            jax.ShapeDtypeStruct((CHUNKS, 8, 48, 128), BF),
        ),
        in_specs=[anywhere] * 6,
        out_specs=(vmem, vmem, vmem),
        scratch_shapes=scratch,
        compiler_params=pltpu.CompilerParams(
            collective_id=0, has_side_effects=True, vmem_limit_bytes=56 * 1024 * 1024
        ),
        name="relations",
    )(
        teacher_query[0],
        teacher_key[0],
        student_hidden[0],
        weight_query,
        weight_key,
        doc_lengths,
    )
    smem = pl.BlockSpec(memory_space=pltpu.SMEM)
    loss, hidden_grad, grad_wq, grad_wk = pl.pallas_call(
        finish,
        out_shape=(
            jax.ShapeDtypeStruct((1,), F32),
            jax.ShapeDtypeStruct((ROWS, DS), BF),
            jax.ShapeDtypeStruct((96, SW), F32),
            jax.ShapeDtypeStruct((96, SW), F32),
        ),
        in_specs=[smem, vmem, vmem],
        out_specs=(smem, vmem, vmem, vmem),
        name="finish",
    )(loss, hidden_grad, terms)
    return loss, hidden_grad[None], grad_wq, grad_wk


def solution(mesh):
    in_specs = (
        P("dp", "ctx", None),
        P("dp", "ctx", None),
        P("dp", "ctx", None),
        P(),
        P(),
        P("dp", None),
    )
    out_specs = (P("dp"), P("dp", "ctx", None), P("ctx", None), P("ctx", None))
    return jax.shard_map(
        per_device, mesh=mesh, in_specs=in_specs, out_specs=out_specs, check_vma=False
    )
```

```python
import math

import jax
import jax.numpy as jnp
from jax import lax
from jax.experimental import pallas as pl
from jax.experimental.pallas import tpu as pltpu
from jax.sharding import PartitionSpec as P

H = 16
TDH = 128
SDH = 48
DOCS = 8
ROWS = 128
SLOTS = 256
TAIL = 64
DS = 1536
TW = H * TDH
SW = H * SDH
LOSS_SCALE = 1048576.0
MASKED = -1e30
LOG2E = math.log2(math.e)
BF = jnp.bfloat16
F32 = jnp.float32
MESH = pl.DeviceIdType.MESH

CHUNKS = 3
PARTS = 3
FIRST_AXIS = ("x", "y", "z")
TILE_OF_HEAD = {(128 * (t + 1) - 1) // SDH: t for t in range(2 * CHUNKS)}
EXTENT = {"xl": 2, "z": 4, "y": 4, "xh": 2}
UNIT = (16, 128)
GROUPS_OF_HEADS = ((0, 2), (2, 6), (6, 10), (10, 13), (13, 16))


def dims_of(axis):
    return ("xl", "xh") if axis == "x" else (axis,)


def left_after(axis):
    return tuple(d for d in ("xl", "z", "y", "xh") if d not in dims_of(axis))


def extent(dims):
    return tuple(EXTENT[d] for d in dims)


def kernel(
    tq,
    tk,
    hid,
    wq,
    wk,
    lengths_in,
    out_loss,
    out_hidden,
    out_terms,
    lengths,
    T,
    Ttail,
    Hd,
    Htail,
    HdT,
    Wown,
    Woth,
    S,
    X,
    E,
    G,
    Gb,
    GX,
    GT,
    Wb,
    agbuf,
    final,
    lossb,
    lossr,
    spare,
    *rest,
):
    pieces = CHUNKS * PARTS
    terms_of, halved, in_line, in_plane = (
        rest[i * pieces : (i + 1) * pieces] for i in range(4)
    )
    loc, tail_s, tail_r, rs_s, rs_r, ag_s, ag_r, loss_s, loss_r = rest[4 * pieces :]

    dp = lax.axis_index("dp")
    ctx = lax.axis_index("ctx")
    y, xh = lax.div(dp, 2), lax.rem(dp, 2)
    core = lax.rem(ctx, 2)
    k = lax.div(ctx, 2)
    z, xl = lax.rem(k, 4), lax.div(k, 4)
    x = xh * 2 + xl
    coords = {"x": x, "y": y, "z": z}

    def device(x_, y_, z_, core_):
        return {"dp": y_ * 2 + lax.div(x_, 2), "ctx": (lax.rem(x_, 2) * 4 + z_) * 2 + core_}

    def along(axis, j):
        c = dict(coords)
        c[axis] = lax.rem(c[axis] + j, 4)
        return device(c["x"], c["y"], c["z"], core), c[axis]

    pair = {"dp": dp, "ctx": k * 2 + 1 - core}
    is0, is1 = core == 0, core == 1
    has_next, has_prev = k < 7, k > 0
    sends = jnp.logical_and(is1, has_next)

    mine = pl.ds(pl.multiple_of(core * ROWS, ROWS), ROWS)
    theirs = pl.ds(pl.multiple_of((1 - core) * ROWS, ROWS), ROWS)
    own_hidden = pltpu.make_async_copy(hid, Hd.at[mine], loc.at[0])
    own_hidden.start()
    get_lengths = pltpu.make_async_copy(lengths_in, lengths, loc.at[4])
    get_lengths.start()

    def by_core(first, second, dst, sem):
        def go(src):
            def start():
                pltpu.make_async_copy(src, dst, sem).start()

            return start

        pl.when(is0)(go(first))
        pl.when(is1)(go(second))
        return pltpu.make_async_copy(first, dst, sem)

    w_own = by_core(wq, wk, Wown, loc.at[1])
    own_t = by_core(tq, tk, T.at[mine], loc.at[2])
    w_oth = by_core(wk, wq, Woth, loc.at[3])

    barrier = pltpu.get_barrier_semaphore()

    def hail(device_id):
        pl.semaphore_signal(barrier, inc=1, device_id=device_id, device_id_type=MESH)

    hail(pair)
    for axis in ("x", "y", "z"):
        for j in (1, 2, 3):
            hail(along(axis, j)[0])

    @pl.when(sends)
    def _():
        hail({"dp": dp, "ctx": k * 2 + 2})
        hail({"dp": dp, "ctx": k * 2 + 3})

    @pl.when(has_prev)
    def _():
        hail({"dp": dp, "ctx": k * 2 - 1})

    pl.semaphore_wait(
        barrier, 10 + jnp.where(sends, 2, 0) + jnp.where(has_prev, 1, 0)
    )

    pending = []

    def copy_of(src, dst, send_sem, recv_sem, device_id):
        return pltpu.make_async_remote_copy(
            src_ref=src,
            dst_ref=dst,
            send_sem=send_sem,
            recv_sem=recv_sem,
            device_id=device_id,
            device_id_type=MESH,
        )

    def when(cond, act):
        if cond is None:
            act()
        else:
            pl.when(cond)(act)

    def remote(src, dst, send_sem, recv_sem, device_id, cond=None):
        when(cond, copy_of(src, dst, send_sem, recv_sem, device_id).start)

    def sent(like, send_sem, cond=None):
        pending.append((copy_of(like, like, send_sem, send_sem, pair), cond))

    def arrived(dst, recv_sem, cond=None):
        when(cond, copy_of(dst, dst, recv_sem, recv_sem, pair).wait_recv)

    last = pl.ds(ROWS - TAIL, TAIL)
    half = DS // 2
    for c in range(2):
        cols = pl.ds(c * half, half)
        remote(
            hid.at[last, cols],
            Htail.at[:, cols],
            tail_s.at[1],
            tail_r.at[1],
            {"dp": dp, "ctx": k * 2 + 2 + c},
            sends,
        )
    sent(Htail, tail_s.at[1], sends)
    remote(hid, Hd.at[mine], tail_s.at[0], tail_r.at[0], pair)
    sent(Hd.at[mine], tail_s.at[0])
    for q, (h0, h1) in enumerate(GROUPS_OF_HEADS):
        cols = pl.ds(TDH * h0, TDH * (h1 - h0))
        for c, src in enumerate((tq, tk)):
            remote(
                src.at[last, cols],
                Ttail.at[:, cols],
                tail_s.at[3],
                tail_r.at[3 + q],
                {"dp": dp, "ctx": k * 2 + 2 + c},
                sends,
            )
    sent(T.at[mine], tail_s.at[3], sends)
    remote(tk, T.at[mine], tail_s.at[2], tail_r.at[2], pair, is0)
    remote(tq, T.at[mine], tail_s.at[2], tail_r.at[2], pair, is1)
    sent(T.at[mine], tail_s.at[2])

    get_lengths.wait()
    start = jnp.int32(0)
    end = jnp.int32(0)
    count = jnp.int32(0)
    for i in range(DOCS):
        value = lengths[0, i]
        start = start + jnp.where(i < k, value, 0)
        end = end + jnp.where(i <= k, value, 0)
        count = count + value
    lo = end - SLOTS * k
    hi = start - SLOTS * (k - 1)
    mean_over = 1.0 / (H * jnp.full((1, 128), count, jnp.int32).astype(F32))
    coefficient = LOSS_SCALE * mean_over

    def slot(shape, first):
        return lax.broadcasted_iota(jnp.int32, shape, 0) + first

    def tail_mask(width):
        return slot((TAIL, width), SLOTS - TAIL) >= hi

    own_hidden.wait()
    w_own.wait()
    arrived(Hd.at[theirs], tail_r.at[0])
    for r in range(0, SLOTS, 128):
        S[r : r + 128, :] = jnp.dot(
            Hd[r : r + 128, :], Wown[...], preferred_element_type=F32
        ).astype(BF)
    for r in range(0, DS, 128):
        HdT[r : r + 128, :ROWS] = Hd[:ROWS, r : r + 128].T
    my_half = Htail.at[:, pl.ds(pl.multiple_of(core * half, half), half)]
    arrived(my_half, tail_r.at[1], has_prev)
    remote(my_half, my_half, tail_s.at[4], tail_r.at[11], pair, has_prev)
    sent(my_half, tail_s.at[4], has_prev)
    other_half = Htail.at[:, pl.ds(pl.multiple_of((1 - core) * half, half), half)]
    arrived(other_half, tail_r.at[11], has_prev)
    tail_rows = slice(SLOTS - TAIL, SLOTS)
    projected = jnp.dot(Htail[...], Wown[...], preferred_element_type=F32).astype(BF)
    S[tail_rows, :] = jnp.where(tail_mask(SW), projected, S[tail_rows, :])

    own_t.wait()
    arrived(T.at[theirs], tail_r.at[2])

    row_slot = lax.broadcasted_iota(jnp.int32, (SLOTS, 128), 0)
    row_lane = lax.broadcasted_iota(jnp.int32, (SLOTS, 128), 1)
    row_bad = jnp.logical_and(row_slot >= lo, row_slot < hi)
    row_bias = jnp.where(row_bad, MASKED, 0.0)
    bias_tile = jnp.where(row_lane == 0, row_bias, 0.0).astype(BF)
    one_tile = jnp.where(row_lane == 0, 1.0, 0.0).astype(BF)
    bias_all = row_bias.astype(BF)
    rate = []
    for cb in range(2):
        lane_slot = lax.broadcasted_iota(jnp.int32, (1, 128), 1) + 128 * cb
        good = jnp.logical_or(lane_slot < lo, lane_slot >= hi)
        rate.append(jnp.where(good, coefficient, 0.0))
    ct = LOG2E / math.sqrt(TDH)
    cs = LOG2E / math.sqrt(SDH)
    nt = (((1,), (1,)), ((), ()))

    G[...] = jnp.zeros_like(G)

    def probabilities(scores, factor, rate_here):
        high = jnp.max(scores, axis=0, keepdims=True)
        rel = (scores - high) * factor
        raw = jnp.exp2(rel)
        total = jnp.sum(raw, axis=0, keepdims=True)
        return rel, raw * (rate_here / total), jnp.log2(total)

    def student_tiles(h):
        first = SDH * h
        a, b = first // 128, (first + SDH - 1) // 128
        width = (b - a + 1) * 128
        cols = slice(128 * a, 128 * a + width)
        st = S[:, cols]
        lane = lax.broadcasted_iota(jnp.int32, (SLOTS, width), 1) + 128 * a
        inside = jnp.logical_and(lane >= first, lane < first + SDH)
        free = 128 * a if first > 128 * a else 128 * a + width - 1
        return cols, st, jnp.where(inside, st, jnp.zeros_like(st)), lane == free

    def scores(h):
        th = T[:, TDH * h : TDH * (h + 1)]
        X[h % 2] = lax.dot_general(
            jnp.concatenate([th, bias_tile], axis=1),
            jnp.concatenate([th, one_tile], axis=1),
            nt,
            preferred_element_type=F32,
        )
        _, st, picked, free = student_tiles(h)
        bias = jnp.concatenate([bias_all] * (st.shape[1] // 128), axis=1)
        X[2 + h % 2] = lax.dot_general(
            jnp.where(free, bias, picked),
            jnp.where(free, jnp.ones_like(st), st),
            nt,
            preferred_element_type=F32,
        )

    def softmaxes(h, loss):
        for cb in range(2):
            block = slice(128 * cb, 128 * (cb + 1))
            rel_t, et, log_t = probabilities(X[h % 2, :, block], ct, rate[cb])
            rel_s, es, log_s = probabilities(X[2 + h % 2, :, block], cs, rate[cb])
            E[h % 2, :, block] = es - et
            loss = loss + jnp.sum(et * (rel_t - rel_s), axis=0, keepdims=True)
            loss = loss - rate[cb] * (log_t - log_s)
        return loss

    def weigh(h):
        e, w = E.at[h % 2], Wb.at[h % 2]
        cross = e[:128, 128:] + e[128:, :128].T
        for b in range(2):
            block = slice(128 * b, 128 * (b + 1))
            square = e[block, block]
            w[block, block] = (square + square.T).astype(BF)
        w[:128, 128:] = cross.astype(BF)
        w[128:, :128] = cross.T.astype(BF)

    def gradient(h):
        cols, _, picked, _ = student_tiles(h)
        G[:, cols] += jnp.dot(Wb[h % 2], picked, preferred_element_type=F32)

    def at_peer(dims, place):
        index = []
        for d in dims:
            if d in ("xl", "xh"):
                at = place.get("x")
                index.append(
                    slice(None) if at is None else lax.rem(at, 2) if d == "xl" else lax.div(at, 2)
                )
            else:
                index.append(place.get(d, slice(None)))
        return tuple(index)

    def peer_of(offsets):
        place = {a: lax.rem(coords[a] + j, 4) for a, j in offsets.items()}
        full = dict(coords, **place)
        return device(full["x"], full["y"], full["z"], core), place

    ALL_DIMS = ("xl", "z", "y", "xh")

    def send_line(c, p, half_):
        axis, n = FIRST_AXIS[p], c * PARTS + p
        for j in (2, 1, 3):
            peer, place = peer_of({axis: j})
            index = at_peer(ALL_DIMS, place)
            dst = in_line[n].at[j - 1]
            if axis == "x":
                cond = lax.div(place["x"], 2) == half_
            else:
                cond = None
                index = index[:3] + (half_,)
                dst = dst.at[:, :, half_]
            remote(terms_of[n].at[index], dst, rs_s.at[2 * n], rs_r.at[2 * n], peer, cond)

    def sum_line(c, p):
        axis, n = FIRST_AXIS[p], c * PARTS + p
        sent(in_line[n], rs_s.at[2 * n])
        own = terms_of[n].at[at_peer(ALL_DIMS, {axis: coords[axis]})]
        arrived(in_line[n], rs_r.at[2 * n])
        total = own[...].astype(F32)
        for j in range(3):
            total = total + in_line[n][j].astype(F32)
        halved[n][...] = total.astype(BF)

    def send_plane(c, p):
        axis, n = FIRST_AXIS[p], c * PARTS + p
        u, v = (a for a in ("x", "y", "z") if a != axis)
        for ju in (2, 1, 3, 0):
            for jv in (2, 1, 3, 0):
                if ju or jv:
                    peer, place = peer_of({u: ju, v: jv})
                    remote(
                        halved[n].at[at_peer(left_after(axis), place)],
                        in_plane[n].at[ju * 4 + jv - 1],
                        rs_s.at[2 * n + 1],
                        rs_r.at[2 * n + 1],
                        peer,
                    )
        sent(in_plane[n], rs_s.at[2 * n + 1])

    def sum_plane(c, p):
        axis, n = FIRST_AXIS[p], c * PARTS + p
        place = {a: coords[a] for a in ("x", "y", "z") if a != axis}
        arrived(in_plane[n], rs_r.at[2 * n + 1])
        total = halved[n][at_peer(left_after(axis), place)].astype(F32)
        for j in range(15):
            total = total + in_plane[n][j].astype(F32)
        final[c, 16 * p : 16 * (p + 1)] = total.astype(BF)

    def after_line(c):
        for p in range(PARTS):
            sum_line(c, p)
            if c:
                send_plane(c, p)
        if c == 0:
            for p in range(PARTS):
                send_plane(c, p)

    def after_plane(c):
        for p in range(PARTS):
            sum_plane(c, p)
            if c == CHUNKS - 1:
                send_final(c, 16 * p, 16 * (p + 1))
        if c < CHUNKS - 1:
            send_final(c, 0, 48)
        sent(spare, ag_s.at[c], core == goal)
        sent(agbuf.at[c], ag_s.at[c], core != goal)

    def tile_terms(t):
        c, half_ = t // 2, t % 2
        cols = slice(128 * t, 128 * (t + 1))
        Gb[:, cols] = (G[:, cols] * (1.0 / math.sqrt(SDH))).astype(BF)
        for xl_ in range(2):
            terms = (
                jnp.dot(HdT[768 * xl_ : 768 * (xl_ + 1), :], Gb[:, cols], preferred_element_type=F32)
                .astype(BF)
                .reshape(4, 4, PARTS, 16, 128)
            )
            for p in range(PARTS):
                terms_of[c * PARTS + p][xl_, :, :, half_] = terms[:, :, p]
        for p in range(PARTS):
            send_line(c, p, half_)

    yl = lax.rem(y, 2)
    goal = lax.div(y, 2)

    own_block = core * 4 + yl * 2 + xh

    def send_final(c, first, stop):
        rows = pl.ds(first, stop - first)
        for j in (4, 5, 3, 2, 6, 1, 7, 0):
            remote(
                final.at[c, rows],
                agbuf.at[c, own_block, rows],
                ag_s.at[c],
                ag_r.at[c],
                {"dp": lax.rem(dp + j, 8), "ctx": k * 2 + goal},
                None if j else core != goal,
            )

        @pl.when(core == goal)
        def _():
            agbuf[c, own_block, first:stop] = final[c, first:stop]

    loss = jnp.zeros((1, 128), F32)
    def group_arrives(q):
        h0, h1 = GROUPS_OF_HEADS[q]
        cols = slice(TDH * h0, TDH * h1)
        arrived(Ttail.at[:, cols], tail_r.at[3 + q], has_prev)
        T[tail_rows, cols] = jnp.where(
            tail_mask(TDH * (h1 - h0)), Ttail[:, cols], T[tail_rows, cols]
        )

    starts = [h0 for h0, _ in GROUPS_OF_HEADS]
    group_arrives(0)
    scores(0)
    for h in range(H + 1):
        if h + 1 in starts:
            group_arrives(starts.index(h + 1))
        if h + 1 < H:
            scores(h + 1)
        if h:
            gradient(h - 1)
        if h < H:
            loss = softmaxes(h, loss)
            weigh(h)
        if h == 2:
            Hd[tail_rows, :] = jnp.where(tail_mask(DS), Htail[...], Hd[tail_rows, :])
            for r in range(0, DS, 128):
                HdT[r : r + 128, ROWS:] = Hd[ROWS:, r : r + 128].T
        if h - 1 in TILE_OF_HEAD:
            tile_terms(TILE_OF_HEAD[h - 1])

    lossb[0] = jnp.broadcast_to(loss, (8, 128))
    for j in (1, 2, 3):
        remote(lossb.at[0], lossr.at[j - 1], loss_s.at[0], loss_r.at[0], along("z", j)[0])
    sent(lossr.at[0:3], loss_s.at[0])

    after_line(0)

    remote(Gb.at[theirs], GX, tail_s.at[5], tail_r.at[8], pair)
    sent(GX, tail_s.at[5])
    remote(
        Gb.at[tail_rows],
        GT.at[core],
        tail_s.at[6],
        tail_r.at[9 + core],
        {"dp": dp, "ctx": k * 2 - 1},
        has_prev,
    )
    sent(GT.at[0], tail_s.at[6], has_prev)

    after_line(1)
    after_line(2)
    arrived(lossr.at[0:3], loss_r.at[0])
    lossb[1] = lossb[0] + lossr[0] + lossr[1] + lossr[2]
    x_other = xh * 2 + 1 - xl
    remote(lossb.at[1], lossr.at[3], loss_s.at[1], loss_r.at[1], device(x_other, y, z, core))
    sent(lossr.at[3], loss_s.at[1])

    after_plane(0)
    after_plane(1)

    arrived(lossr.at[3], loss_r.at[1])
    lossb[2] = lossb[1] + lossr[3]
    remote(lossb.at[2], lossr.at[4], loss_s.at[2], loss_r.at[2], pair)
    sent(lossr.at[4], loss_s.at[2])

    after_plane(2)

    w_oth.wait()
    arrived(GX, tail_r.at[8])
    for c in range(2):
        arrived(GT.at[c], tail_r.at[9 + c], sends)
    rows = slice(ROWS - TAIL, ROWS)
    lent = slot((TAIL, SW), SLOTS - TAIL - ROWS + core * ROWS) >= lo
    zero = jnp.zeros((TAIL, SW), BF)
    keep = jnp.full((TAIL, SW), k, jnp.int32) < 7
    own_low = Gb[pl.ds(pl.multiple_of(core * ROWS, ROWS), ROWS - TAIL), :]
    own_high = Gb[pl.ds(pl.multiple_of(core * ROWS + ROWS - TAIL, TAIL), TAIL), :]
    own_high = jnp.where(lent, jnp.where(keep, GT[1], zero), own_high)
    GX[rows, :] = jnp.where(lent, jnp.where(keep, GT[0], zero), GX[rows, :])
    own_rows = jnp.concatenate([own_low, own_high], axis=0)
    for r in range(0, DS, 512):
        out_hidden[:, r : r + 512] = (
            lax.dot_general(own_rows, Wown[r : r + 512, :], nt, preferred_element_type=F32)
            + lax.dot_general(GX[...], Woth[r : r + 512, :], nt, preferred_element_type=F32)
        ).astype(BF)

    arrived(lossr.at[4], loss_r.at[2])
    loss_total = lossb[2] + lossr[4]
    out_loss[...] = jnp.broadcast_to(
        jnp.sum(loss_total[:1], axis=1, keepdims=True) * (math.log(2.0) / LOSS_SCALE), (1, 128)
    )

    for c in range(CHUNKS):
        arrived(spare, ag_r.at[c], core == goal)
        arrived(agbuf.at[c], ag_r.at[c], core != goal)
        out_terms[c] = agbuf[c]

    for copy, cond in pending:
        if cond is None:
            copy.wait_send()
        else:
            pl.when(cond)(copy.wait_send)


def finish(loss, hidden_grad, terms, out_loss, out_hidden, out_wq, out_wk):
    out_loss[0] = loss[0, 0]
    out_hidden[...] = hidden_grad[...]
    for r, out in enumerate((out_wq, out_wk)):
        for c in range(CHUNKS):
            for yl in range(2):
                for xh in range(2):
                    at = 256 * c + 128 * xh
                    block = terms[c, r * 4 + yl * 2 + xh]
                    out[48 * yl : 48 * (yl + 1), at : at + 128] = block.astype(F32)


def per_device(teacher_query, teacher_key, student_hidden, weight_query, weight_key, doc_lengths):
    scratch = [
        pltpu.SMEM((1, DOCS), jnp.int32),
        pltpu.VMEM((SLOTS, TW), BF),
        pltpu.VMEM((TAIL, TW), BF),
        pltpu.VMEM((SLOTS, DS), BF),
        pltpu.VMEM((TAIL, DS), BF),
        pltpu.VMEM((DS, SLOTS), BF),
        pltpu.VMEM((DS, SW), BF),
        pltpu.VMEM((DS, SW), BF),
        pltpu.VMEM((SLOTS, SW), BF),
        pltpu.VMEM((4, SLOTS, SLOTS), F32),
        pltpu.VMEM((2, SLOTS, SLOTS), F32),
        pltpu.VMEM((SLOTS, SW), F32),
        pltpu.VMEM((SLOTS, SW), BF),
        pltpu.VMEM((ROWS, SW), BF),
        pltpu.VMEM((2, TAIL, SW), BF),
        pltpu.VMEM((2, SLOTS, SLOTS), BF),
        pltpu.VMEM((CHUNKS, 8, 48, 128), BF),
        pltpu.VMEM((CHUNKS, 48, 128), BF),
        pltpu.VMEM((3, 8, 128), F32),
        pltpu.VMEM((5, 8, 128), F32),
        pltpu.VMEM((7, 48, 128), BF),
    ]
    firsts = FIRST_AXIS * CHUNKS
    for _ in firsts:
        scratch.append(pltpu.VMEM(extent(("xl", "z", "y", "xh")) + UNIT, BF))
    for axis in firsts:
        scratch.append(pltpu.VMEM(extent(left_after(axis)) + UNIT, BF))
    for axis in firsts:
        scratch.append(pltpu.VMEM((3,) + extent(left_after(axis)) + UNIT, BF))
    for _ in firsts:
        scratch.append(pltpu.VMEM((15,) + UNIT, BF))
    dma = pltpu.SemaphoreType.DMA
    scratch += [
        dma((5,)),
        dma((7,)),
        dma((12,)),
        dma((18,)),
        dma((18,)),
        dma((3,)),
        dma((3,)),
        dma((3,)),
        dma((3,)),
    ]
    vmem = pl.BlockSpec(memory_space=pltpu.VMEM)
    anywhere = pl.BlockSpec(memory_space=pl.ANY)
    loss, hidden_grad, terms = pl.pallas_call(
        kernel,
        out_shape=(
            jax.ShapeDtypeStruct((1, 128), F32),
            jax.ShapeDtypeStruct((ROWS, DS), BF),
            jax.ShapeDtypeStruct((CHUNKS, 8, 48, 128), BF),
        ),
        in_specs=[anywhere] * 6,
        out_specs=(vmem, vmem, vmem),
        scratch_shapes=scratch,
        compiler_params=pltpu.CompilerParams(
            collective_id=0, has_side_effects=True, vmem_limit_bytes=56 * 1024 * 1024
        ),
        name="relations",
    )(
        teacher_query[0],
        teacher_key[0],
        student_hidden[0],
        weight_query,
        weight_key,
        doc_lengths,
    )
    smem = pl.BlockSpec(memory_space=pltpu.SMEM)
    loss, hidden_grad, grad_wq, grad_wk = pl.pallas_call(
        finish,
        out_shape=(
            jax.ShapeDtypeStruct((1,), F32),
            jax.ShapeDtypeStruct((ROWS, DS), BF),
            jax.ShapeDtypeStruct((96, SW), F32),
            jax.ShapeDtypeStruct((96, SW), F32),
        ),
        in_specs=[smem, vmem, vmem],
        out_specs=(smem, vmem, vmem, vmem),
        name="finish",
    )(loss, hidden_grad, terms)
    return loss, hidden_grad[None], grad_wq, grad_wk


def solution(mesh):
    in_specs = (
        P("dp", "ctx", None),
        P("dp", "ctx", None),
        P("dp", "ctx", None),
        P(),
        P(),
        P("dp", None),
    )
    out_specs = (P("dp"), P("dp", "ctx", None), P("ctx", None), P("ctx", None))
    return jax.shard_map(
        per_device, mesh=mesh, in_specs=in_specs, out_specs=out_specs, check_vma=False
    )
```

```python
import math

import jax
import jax.numpy as jnp
from jax import lax
from jax.experimental import pallas as pl
from jax.experimental.pallas import tpu as pltpu
from jax.sharding import PartitionSpec as P

H = 16
TDH = 128
SDH = 48
DOCS = 8
ROWS = 128
SLOTS = 256
TAIL = 64
DS = 1536
TW = H * TDH
SW = H * SDH
LOSS_SCALE = 1048576.0
MASKED = -1e30
LOG2E = math.log2(math.e)
BF = jnp.bfloat16
F32 = jnp.float32
MESH = pl.DeviceIdType.MESH

CHUNKS = 3
PARTS = 3
FIRST_AXIS = ("x", "y", "z")
TILE_OF_HEAD = {(128 * (t + 1) - 1) // SDH: t for t in range(2 * CHUNKS)}
EXTENT = {"xl": 2, "z": 4, "y": 4, "xh": 2}
UNIT = (16, 128)
GROUPS_OF_HEADS = ((0, 2), (2, 6), (6, 10), (10, 13), (13, 16))


def dims_of(axis):
    return ("xl", "xh") if axis == "x" else (axis,)


def left_after(axis):
    return tuple(d for d in ("xl", "z", "y", "xh") if d not in dims_of(axis))


def extent(dims):
    return tuple(EXTENT[d] for d in dims)


def kernel(
    tq,
    tk,
    hid,
    wq,
    wk,
    lengths_in,
    out_loss,
    out_hidden,
    out_terms,
    lengths,
    T,
    Ttail,
    Hd,
    Htail,
    HdT,
    Wown,
    Woth,
    S,
    X,
    E,
    G,
    Gb,
    GX,
    GT,
    Wb,
    hidden_rows,
    agbuf,
    final,
    lossb,
    lossr,
    spare,
    *rest,
):
    pieces = CHUNKS * PARTS
    terms_of, halved, in_line, in_plane = (
        rest[i * pieces : (i + 1) * pieces] for i in range(4)
    )
    loc, tail_s, tail_r, rs_s, rs_r, ag_s, ag_r, loss_s, loss_r = rest[4 * pieces :]

    dp = lax.axis_index("dp")
    ctx = lax.axis_index("ctx")
    y, xh = lax.div(dp, 2), lax.rem(dp, 2)
    core = lax.rem(ctx, 2)
    k = lax.div(ctx, 2)
    z, xl = lax.rem(k, 4), lax.div(k, 4)
    x = xh * 2 + xl
    coords = {"x": x, "y": y, "z": z}

    def device(x_, y_, z_, core_):
        return {"dp": y_ * 2 + lax.div(x_, 2), "ctx": (lax.rem(x_, 2) * 4 + z_) * 2 + core_}

    def along(axis, j):
        c = dict(coords)
        c[axis] = lax.rem(c[axis] + j, 4)
        return device(c["x"], c["y"], c["z"], core), c[axis]

    pair = {"dp": dp, "ctx": k * 2 + 1 - core}
    is0, is1 = core == 0, core == 1
    has_next, has_prev = k < 7, k > 0
    sends = jnp.logical_and(is1, has_next)

    mine = pl.ds(pl.multiple_of(core * ROWS, ROWS), ROWS)
    theirs = pl.ds(pl.multiple_of((1 - core) * ROWS, ROWS), ROWS)
    own_hidden = pltpu.make_async_copy(hid, Hd.at[mine], loc.at[0])
    own_hidden.start()
    get_lengths = pltpu.make_async_copy(lengths_in, lengths, loc.at[4])
    get_lengths.start()

    def by_core(first, second, dst, sem):
        def go(src):
            def start():
                pltpu.make_async_copy(src, dst, sem).start()

            return start

        pl.when(is0)(go(first))
        pl.when(is1)(go(second))
        return pltpu.make_async_copy(first, dst, sem)

    w_own = by_core(wq, wk, Wown, loc.at[1])
    own_t = by_core(tq, tk, T.at[mine], loc.at[2])
    w_oth = by_core(wk, wq, Woth, loc.at[3])

    barrier = pltpu.get_barrier_semaphore()

    def hail(device_id):
        pl.semaphore_signal(barrier, inc=1, device_id=device_id, device_id_type=MESH)

    hail(pair)
    for axis in ("x", "y", "z"):
        for j in (1, 2, 3):
            hail(along(axis, j)[0])

    @pl.when(sends)
    def _():
        hail({"dp": dp, "ctx": k * 2 + 2})
        hail({"dp": dp, "ctx": k * 2 + 3})

    @pl.when(has_prev)
    def _():
        hail({"dp": dp, "ctx": k * 2 - 1})

    pl.semaphore_wait(
        barrier, 10 + jnp.where(sends, 2, 0) + jnp.where(has_prev, 1, 0)
    )

    pending = []

    def copy_of(src, dst, send_sem, recv_sem, device_id):
        return pltpu.make_async_remote_copy(
            src_ref=src,
            dst_ref=dst,
            send_sem=send_sem,
            recv_sem=recv_sem,
            device_id=device_id,
            device_id_type=MESH,
        )

    def when(cond, act):
        if cond is None:
            act()
        else:
            pl.when(cond)(act)

    def remote(src, dst, send_sem, recv_sem, device_id, cond=None):
        when(cond, copy_of(src, dst, send_sem, recv_sem, device_id).start)

    def sent(like, send_sem, cond=None):
        pending.append((copy_of(like, like, send_sem, send_sem, pair), cond))

    def arrived(dst, recv_sem, cond=None):
        when(cond, copy_of(dst, dst, recv_sem, recv_sem, pair).wait_recv)

    last = pl.ds(ROWS - TAIL, TAIL)
    half = DS // 2
    for c in range(2):
        cols = pl.ds(c * half, half)
        remote(
            hid.at[last, cols],
            Htail.at[:, cols],
            tail_s.at[1],
            tail_r.at[1],
            {"dp": dp, "ctx": k * 2 + 2 + c},
            sends,
        )
    sent(Htail, tail_s.at[1], sends)
    remote(hid, Hd.at[mine], tail_s.at[0], tail_r.at[0], pair)
    sent(Hd.at[mine], tail_s.at[0])
    for q, (h0, h1) in enumerate(GROUPS_OF_HEADS):
        cols = pl.ds(TDH * h0, TDH * (h1 - h0))
        for c, src in enumerate((tq, tk)):
            remote(
                src.at[last, cols],
                Ttail.at[:, cols],
                tail_s.at[3],
                tail_r.at[3 + q],
                {"dp": dp, "ctx": k * 2 + 2 + c},
                sends,
            )
    sent(T.at[mine], tail_s.at[3], sends)
    remote(tk, T.at[mine], tail_s.at[2], tail_r.at[2], pair, is0)
    remote(tq, T.at[mine], tail_s.at[2], tail_r.at[2], pair, is1)
    sent(T.at[mine], tail_s.at[2])

    get_lengths.wait()
    start = jnp.int32(0)
    end = jnp.int32(0)
    count = jnp.int32(0)
    for i in range(DOCS):
        value = lengths[0, i]
        start = start + jnp.where(i < k, value, 0)
        end = end + jnp.where(i <= k, value, 0)
        count = count + value
    lo = end - SLOTS * k
    hi = start - SLOTS * (k - 1)
    mean_over = 1.0 / (H * jnp.full((1, 128), count, jnp.int32).astype(F32))
    coefficient = LOSS_SCALE * mean_over

    def slot(shape, first):
        return lax.broadcasted_iota(jnp.int32, shape, 0) + first

    def tail_mask(width):
        return slot((TAIL, width), SLOTS - TAIL) >= hi

    own_hidden.wait()
    w_own.wait()
    arrived(Hd.at[theirs], tail_r.at[0])
    for r in range(0, SLOTS, 128):
        S[r : r + 128, :] = jnp.dot(
            Hd[r : r + 128, :], Wown[...], preferred_element_type=F32
        ).astype(BF)
    for r in range(0, DS, 128):
        HdT[r : r + 128, :ROWS] = Hd[:ROWS, r : r + 128].T
    my_half = Htail.at[:, pl.ds(pl.multiple_of(core * half, half), half)]
    arrived(my_half, tail_r.at[1], has_prev)
    remote(my_half, my_half, tail_s.at[4], tail_r.at[11], pair, has_prev)
    sent(my_half, tail_s.at[4], has_prev)
    other_half = Htail.at[:, pl.ds(pl.multiple_of((1 - core) * half, half), half)]
    arrived(other_half, tail_r.at[11], has_prev)
    tail_rows = slice(SLOTS - TAIL, SLOTS)
    projected = jnp.dot(Htail[...], Wown[...], preferred_element_type=F32).astype(BF)
    S[tail_rows, :] = jnp.where(tail_mask(SW), projected, S[tail_rows, :])

    own_t.wait()
    arrived(T.at[theirs], tail_r.at[2])

    row_slot = lax.broadcasted_iota(jnp.int32, (SLOTS, 128), 0)
    row_lane = lax.broadcasted_iota(jnp.int32, (SLOTS, 128), 1)
    row_bad = jnp.logical_and(row_slot >= lo, row_slot < hi)
    row_bias = jnp.where(row_bad, MASKED, 0.0)
    bias_tile = jnp.where(row_lane == 0, row_bias, 0.0).astype(BF)
    one_tile = jnp.where(row_lane == 0, 1.0, 0.0).astype(BF)
    bias_all = row_bias.astype(BF)
    rate = []
    for cb in range(2):
        lane_slot = lax.broadcasted_iota(jnp.int32, (1, 128), 1) + 128 * cb
        good = jnp.logical_or(lane_slot < lo, lane_slot >= hi)
        rate.append(jnp.where(good, coefficient, 0.0))
    ct = LOG2E / math.sqrt(TDH)
    cs = LOG2E / math.sqrt(SDH)
    nt = (((1,), (1,)), ((), ()))

    G[...] = jnp.zeros_like(G)

    def probabilities(scores, factor, rate_here):
        high = jnp.max(scores, axis=0, keepdims=True)
        rel = (scores - high) * factor
        raw = jnp.exp2(rel)
        total = jnp.sum(raw, axis=0, keepdims=True)
        return rel, raw * (rate_here / total), jnp.log2(total)

    def student_tiles(h):
        first = SDH * h
        a, b = first // 128, (first + SDH - 1) // 128
        width = (b - a + 1) * 128
        cols = slice(128 * a, 128 * a + width)
        st = S[:, cols]
        lane = lax.broadcasted_iota(jnp.int32, (SLOTS, width), 1) + 128 * a
        inside = jnp.logical_and(lane >= first, lane < first + SDH)
        free = 128 * a if first > 128 * a else 128 * a + width - 1
        return cols, st, jnp.where(inside, st, jnp.zeros_like(st)), lane == free

    def scores(h):
        th = T[:, TDH * h : TDH * (h + 1)]
        X[h % 2] = lax.dot_general(
            jnp.concatenate([th, bias_tile], axis=1),
            jnp.concatenate([th, one_tile], axis=1),
            nt,
            preferred_element_type=F32,
        )
        _, st, picked, free = student_tiles(h)
        bias = jnp.concatenate([bias_all] * (st.shape[1] // 128), axis=1)
        X[2 + h % 2] = lax.dot_general(
            jnp.where(free, bias, picked),
            jnp.where(free, jnp.ones_like(st), st),
            nt,
            preferred_element_type=F32,
        )

    def softmaxes(h, loss):
        for cb in range(2):
            block = slice(128 * cb, 128 * (cb + 1))
            rel_t, et, log_t = probabilities(X[h % 2, :, block], ct, rate[cb])
            rel_s, es, log_s = probabilities(X[2 + h % 2, :, block], cs, rate[cb])
            E[h % 2, :, block] = es - et
            loss = loss + jnp.sum(et * (rel_t - rel_s), axis=0, keepdims=True)
            loss = loss - rate[cb] * (log_t - log_s)
        return loss

    def weigh(h):
        e, w = E.at[h % 2], Wb.at[h % 2]
        cross = e[:128, 128:] + e[128:, :128].T
        for b in range(2):
            block = slice(128 * b, 128 * (b + 1))
            square = e[block, block]
            w[block, block] = (square + square.T).astype(BF)
        w[:128, 128:] = cross.astype(BF)
        w[128:, :128] = cross.T.astype(BF)

    def gradient(h):
        cols, _, picked, _ = student_tiles(h)
        G[:, cols] += jnp.dot(Wb[h % 2], picked, preferred_element_type=F32)

    def at_peer(dims, place):
        index = []
        for d in dims:
            if d in ("xl", "xh"):
                at = place.get("x")
                index.append(
                    slice(None) if at is None else lax.rem(at, 2) if d == "xl" else lax.div(at, 2)
                )
            else:
                index.append(place.get(d, slice(None)))
        return tuple(index)

    def peer_of(offsets):
        place = {a: lax.rem(coords[a] + j, 4) for a, j in offsets.items()}
        full = dict(coords, **place)
        return device(full["x"], full["y"], full["z"], core), place

    ALL_DIMS = ("xl", "z", "y", "xh")

    def send_line(c, p, half_):
        axis, n = FIRST_AXIS[p], c * PARTS + p
        for j in (2, 1, 3):
            peer, place = peer_of({axis: j})
            index = at_peer(ALL_DIMS, place)
            dst = in_line[n].at[j - 1]
            if axis == "x":
                cond = lax.div(place["x"], 2) == half_
            else:
                cond = None
                index = index[:3] + (half_,)
                dst = dst.at[:, :, half_]
            remote(terms_of[n].at[index], dst, rs_s.at[2 * n], rs_r.at[2 * n], peer, cond)

    def sum_line(c, p):
        axis, n = FIRST_AXIS[p], c * PARTS + p
        sent(in_line[n], rs_s.at[2 * n])
        own = terms_of[n].at[at_peer(ALL_DIMS, {axis: coords[axis]})]
        arrived(in_line[n], rs_r.at[2 * n])
        total = own[...].astype(F32)
        for j in range(3):
            total = total + in_line[n][j].astype(F32)
        halved[n][...] = total.astype(BF)

    def send_plane(c, p):
        axis, n = FIRST_AXIS[p], c * PARTS + p
        u, v = (a for a in ("x", "y", "z") if a != axis)
        for ju in (2, 1, 3, 0):
            for jv in (2, 1, 3, 0):
                if ju or jv:
                    peer, place = peer_of({u: ju, v: jv})
                    remote(
                        halved[n].at[at_peer(left_after(axis), place)],
                        in_plane[n].at[ju * 4 + jv - 1],
                        rs_s.at[2 * n + 1],
                        rs_r.at[2 * n + 1],
                        peer,
                    )
        sent(in_plane[n], rs_s.at[2 * n + 1])

    def sum_plane(c, p):
        axis, n = FIRST_AXIS[p], c * PARTS + p
        place = {a: coords[a] for a in ("x", "y", "z") if a != axis}
        arrived(in_plane[n], rs_r.at[2 * n + 1])
        total = halved[n][at_peer(left_after(axis), place)].astype(F32)
        for j in range(15):
            total = total + in_plane[n][j].astype(F32)
        final[c, 16 * p : 16 * (p + 1)] = total.astype(BF)

    def after_line(c):
        for p in range(PARTS):
            sum_line(c, p)
            if c:
                send_plane(c, p)
        if c == 0:
            for p in range(PARTS):
                send_plane(c, p)

    def after_plane(c):
        for p in range(PARTS):
            sum_plane(c, p)
            if c == CHUNKS - 1:
                send_final(c, 16 * p, 16 * (p + 1))
        if c < CHUNKS - 1:
            send_final(c, 0, 48)
        sent(spare, ag_s.at[c], core == goal)
        sent(agbuf.at[c], ag_s.at[c], core != goal)

    def tile_terms(t):
        c, half_ = t // 2, t % 2
        cols = slice(128 * t, 128 * (t + 1))
        Gb[:, cols] = (G[:, cols] * (1.0 / math.sqrt(SDH))).astype(BF)
        for xl_ in range(2):
            terms = (
                jnp.dot(HdT[768 * xl_ : 768 * (xl_ + 1), :], Gb[:, cols], preferred_element_type=F32)
                .astype(BF)
                .reshape(4, 4, PARTS, 16, 128)
            )
            for p in range(PARTS):
                terms_of[c * PARTS + p][xl_, :, :, half_] = terms[:, :, p]
        for p in range(PARTS):
            send_line(c, p, half_)

    yl = lax.rem(y, 2)
    goal = lax.div(y, 2)

    own_block = core * 4 + yl * 2 + xh

    def send_final(c, first, stop):
        rows = pl.ds(first, stop - first)
        for j in (4, 5, 3, 2, 6, 1, 7, 0):
            remote(
                final.at[c, rows],
                agbuf.at[c, own_block, rows],
                ag_s.at[c],
                ag_r.at[c],
                {"dp": lax.rem(dp + j, 8), "ctx": k * 2 + goal},
                None if j else core != goal,
            )

        @pl.when(core == goal)
        def _():
            agbuf[c, own_block, first:stop] = final[c, first:stop]

    loss = jnp.zeros((1, 128), F32)
    def group_arrives(q):
        h0, h1 = GROUPS_OF_HEADS[q]
        cols = slice(TDH * h0, TDH * h1)
        arrived(Ttail.at[:, cols], tail_r.at[3 + q], has_prev)
        T[tail_rows, cols] = jnp.where(
            tail_mask(TDH * (h1 - h0)), Ttail[:, cols], T[tail_rows, cols]
        )

    starts = [h0 for h0, _ in GROUPS_OF_HEADS]
    group_arrives(0)
    scores(0)
    for h in range(H + 1):
        if h + 1 in starts:
            group_arrives(starts.index(h + 1))
        if h + 1 < H:
            scores(h + 1)
        if h:
            gradient(h - 1)
        if h < H:
            loss = softmaxes(h, loss)
            weigh(h)
        if h == 2:
            Hd[tail_rows, :] = jnp.where(tail_mask(DS), Htail[...], Hd[tail_rows, :])
            for r in range(0, DS, 128):
                HdT[r : r + 128, ROWS:] = Hd[ROWS:, r : r + 128].T
        if h - 1 in TILE_OF_HEAD:
            tile_terms(TILE_OF_HEAD[h - 1])

    lossb[0] = jnp.broadcast_to(loss, (8, 128))
    for j in (1, 2, 3):
        remote(lossb.at[0], lossr.at[j - 1], loss_s.at[0], loss_r.at[0], along("z", j)[0])
    sent(lossr.at[0:3], loss_s.at[0])

    after_line(0)

    remote(Gb.at[theirs], GX, tail_s.at[5], tail_r.at[8], pair)
    sent(GX, tail_s.at[5])
    remote(
        Gb.at[tail_rows],
        GT.at[core],
        tail_s.at[6],
        tail_r.at[9 + core],
        {"dp": dp, "ctx": k * 2 - 1},
        has_prev,
    )
    sent(GT.at[0], tail_s.at[6], has_prev)

    after_line(1)
    after_line(2)
    arrived(lossr.at[0:3], loss_r.at[0])
    lossb[1] = lossb[0] + lossr[0] + lossr[1] + lossr[2]
    x_other = xh * 2 + 1 - xl
    remote(lossb.at[1], lossr.at[3], loss_s.at[1], loss_r.at[1], device(x_other, y, z, core))
    sent(lossr.at[3], loss_s.at[1])

    after_plane(0)
    after_plane(1)

    arrived(lossr.at[3], loss_r.at[1])
    lossb[2] = lossb[1] + lossr[3]
    remote(lossb.at[2], lossr.at[4], loss_s.at[2], loss_r.at[2], pair)
    sent(lossr.at[4], loss_s.at[2])

    after_plane(2)

    w_oth.wait()
    arrived(GX, tail_r.at[8])
    for c in range(2):
        arrived(GT.at[c], tail_r.at[9 + c], sends)
    rows = slice(ROWS - TAIL, ROWS)
    lent = slot((TAIL, SW), SLOTS - TAIL - ROWS + core * ROWS) >= lo
    zero = jnp.zeros((TAIL, SW), BF)
    keep = jnp.full((TAIL, SW), k, jnp.int32) < 7
    own_low = Gb[pl.ds(pl.multiple_of(core * ROWS, ROWS), ROWS - TAIL), :]
    own_high = Gb[pl.ds(pl.multiple_of(core * ROWS + ROWS - TAIL, TAIL), TAIL), :]
    own_high = jnp.where(lent, jnp.where(keep, GT[1], zero), own_high)
    GX[rows, :] = jnp.where(lent, jnp.where(keep, GT[0], zero), GX[rows, :])
    own_rows = jnp.concatenate([own_low, own_high], axis=0)
    for r in range(0, DS, 512):
        hidden_rows[:, r : r + 512] = (
            lax.dot_general(own_rows, Wown[r : r + 512, :], nt, preferred_element_type=F32)
            + lax.dot_general(GX[...], Woth[r : r + 512, :], nt, preferred_element_type=F32)
        ).astype(BF)
    kept = [pltpu.make_async_copy(hidden_rows, out_hidden, loc.at[5])]
    kept[0].start()

    arrived(lossr.at[4], loss_r.at[2])
    loss_total = lossb[2] + lossr[4]
    out_loss[...] = jnp.broadcast_to(
        jnp.sum(loss_total[:1], axis=1, keepdims=True) * (math.log(2.0) / LOSS_SCALE), (1, 128)
    )

    for c in range(CHUNKS):
        arrived(spare, ag_r.at[c], core == goal)
        arrived(agbuf.at[c], ag_r.at[c], core != goal)
        kept.append(pltpu.make_async_copy(agbuf.at[c], out_terms.at[c], loc.at[6 + c]))
        kept[-1].start()
    for copy in kept:
        copy.wait()

    for copy, cond in pending:
        if cond is None:
            copy.wait_send()
        else:
            pl.when(cond)(copy.wait_send)


def finish(loss, hidden_grad, terms, out_loss, out_hidden, out_wq, out_wk):
    out_loss[0] = loss[0, 0]
    out_hidden[...] = hidden_grad[...]
    for r, out in enumerate((out_wq, out_wk)):
        for c in range(CHUNKS):
            for yl in range(2):
                for xh in range(2):
                    at = 256 * c + 128 * xh
                    block = terms[c, r * 4 + yl * 2 + xh]
                    out[48 * yl : 48 * (yl + 1), at : at + 128] = block.astype(F32)


def per_device(teacher_query, teacher_key, student_hidden, weight_query, weight_key, doc_lengths):
    scratch = [
        pltpu.SMEM((1, DOCS), jnp.int32),
        pltpu.VMEM((SLOTS, TW), BF),
        pltpu.VMEM((TAIL, TW), BF),
        pltpu.VMEM((SLOTS, DS), BF),
        pltpu.VMEM((TAIL, DS), BF),
        pltpu.VMEM((DS, SLOTS), BF),
        pltpu.VMEM((DS, SW), BF),
        pltpu.VMEM((DS, SW), BF),
        pltpu.VMEM((SLOTS, SW), BF),
        pltpu.VMEM((4, SLOTS, SLOTS), F32),
        pltpu.VMEM((2, SLOTS, SLOTS), F32),
        pltpu.VMEM((SLOTS, SW), F32),
        pltpu.VMEM((SLOTS, SW), BF),
        pltpu.VMEM((ROWS, SW), BF),
        pltpu.VMEM((2, TAIL, SW), BF),
        pltpu.VMEM((2, SLOTS, SLOTS), BF),
        pltpu.VMEM((ROWS, DS), BF),
        pltpu.VMEM((CHUNKS, 8, 48, 128), BF),
        pltpu.VMEM((CHUNKS, 48, 128), BF),
        pltpu.VMEM((3, 8, 128), F32),
        pltpu.VMEM((5, 8, 128), F32),
        pltpu.VMEM((7, 48, 128), BF),
    ]
    firsts = FIRST_AXIS * CHUNKS
    for _ in firsts:
        scratch.append(pltpu.VMEM(extent(("xl", "z", "y", "xh")) + UNIT, BF))
    for axis in firsts:
        scratch.append(pltpu.VMEM(extent(left_after(axis)) + UNIT, BF))
    for axis in firsts:
        scratch.append(pltpu.VMEM((3,) + extent(left_after(axis)) + UNIT, BF))
    for _ in firsts:
        scratch.append(pltpu.VMEM((15,) + UNIT, BF))
    dma = pltpu.SemaphoreType.DMA
    scratch += [
        dma((9,)),
        dma((7,)),
        dma((12,)),
        dma((18,)),
        dma((18,)),
        dma((3,)),
        dma((3,)),
        dma((3,)),
        dma((3,)),
    ]
    vmem = pl.BlockSpec(memory_space=pltpu.VMEM)
    anywhere = pl.BlockSpec(memory_space=pl.ANY)
    loss, hidden_grad, terms = pl.pallas_call(
        kernel,
        out_shape=(
            jax.ShapeDtypeStruct((1, 128), F32),
            jax.ShapeDtypeStruct((ROWS, DS), BF),
            jax.ShapeDtypeStruct((CHUNKS, 8, 48, 128), BF),
        ),
        in_specs=[anywhere] * 6,
        out_specs=(vmem, anywhere, anywhere),
        scratch_shapes=scratch,
        compiler_params=pltpu.CompilerParams(
            collective_id=0, has_side_effects=True, vmem_limit_bytes=56 * 1024 * 1024
        ),
        name="relations",
    )(
        teacher_query[0],
        teacher_key[0],
        student_hidden[0],
        weight_query,
        weight_key,
        doc_lengths,
    )
    smem = pl.BlockSpec(memory_space=pltpu.SMEM)
    loss, hidden_grad, grad_wq, grad_wk = pl.pallas_call(
        finish,
        out_shape=(
            jax.ShapeDtypeStruct((1,), F32),
            jax.ShapeDtypeStruct((ROWS, DS), BF),
            jax.ShapeDtypeStruct((96, SW), F32),
            jax.ShapeDtypeStruct((96, SW), F32),
        ),
        in_specs=[smem, vmem, vmem],
        out_specs=(smem, vmem, vmem, vmem),
        name="finish",
    )(loss, hidden_grad, terms)
    return loss, hidden_grad[None], grad_wq, grad_wk


def solution(mesh):
    in_specs = (
        P("dp", "ctx", None),
        P("dp", "ctx", None),
        P("dp", "ctx", None),
        P(),
        P(),
        P("dp", None),
    )
    out_specs = (P("dp"), P("dp", "ctx", None), P("ctx", None), P("ctx", None))
    return jax.shard_map(
        per_device, mesh=mesh, in_specs=in_specs, out_specs=out_specs, check_vma=False
    )
```
